512 devices in a mesh: head: 8 (over x_hi, y), seq: 64 (over z, x_lo, core).
Axes of the slice: x: 4 (x_hi: 2, x_lo: 2; x = x_hi * 2 + x_lo), y: 4, z: 16, core: 2. Of those that a mesh axis runs over, the one named last changes fastest.
Arguments:
- queries: bfloat16 [8, 16384, 128], P('head', 'seq'), may hold values from -80 to 80
- keys: bfloat16 [8, 24576, 128], P('head', 'seq'), may hold values from -24 to 24
- head_pick: int32 [8], P('head'), may hold values from 0 to 63
- block_offset: int32 [8], P('head'), may hold values from 0 to 64, as said below
- owner_map: int32 [192], replicated, may hold values from 0 to 191, each once
Outputs:
- block_mass: float32 [8, 192, 128], P('head', 'seq')
The draws below stay inside these ranges and needn't reach their ends.
Inputs may be any that keep to these rules, and one draw needn't show every extreme that they name: Query row r of group g stands at prompt position 128 * block_offset[g] + r. `owner_map`: names each key block once.
All inputs are finite; a program needn't handle non-finite values.
Results may differ from the reference program's by a relative error of at most 0.0003.
Values may be sent and summed in bfloat16 or wider, within the bound.
A program may use at most 64 MiB of HBM per device.

```python
import math
import jax
import jax.numpy as jnp
from jax import lax

QH = 64
KV = 8
HD = 128
BLK = 128
Q_DEV = 256
K_DEV = 384
QUERIES = 16384
KEYS = 24576
QBLK = 128
KBLK = 192
N_HEAD = 8
N_SEQ = 64


def structured(noise_key, mean_key, weight_key, heads, length):
    blocks = length // BLK
    noise = jax.random.normal(noise_key, (heads, blocks, BLK, HD), jnp.float32)
    means = jax.random.normal(mean_key, (heads, blocks, 1, HD), jnp.float32)
    weights = jax.random.uniform(weight_key, (heads, blocks, 1, 1), jnp.float32, 0.0, 1.5)
    return (noise + weights * means).reshape(heads, length, HD)


def draw_keys(key, part):
    key = jax.random.fold_in(key, 5)
    noise_key, mean_key, weight_key = jax.random.split(key, 3)
    result = structured(noise_key, mean_key, weight_key, KV, KEYS)
    return result.astype(jnp.bfloat16)


def draw_queries(key, part):
    key = jax.random.fold_in(key, 9)
    noise_key, mean_key, weight_key = jax.random.split(key, 3)
    result = structured(noise_key, mean_key, weight_key, N_HEAD, QUERIES)
    return result.astype(jnp.bfloat16)


def draw_block_offset(key, part):
    key = jax.random.fold_in(key, 37)
    first_key, second_key = jax.random.split(key, 2)
    highest = (K_DEV - Q_DEV) * N_SEQ // BLK
    values = jax.random.randint(first_key, (N_HEAD,), 0, highest + 1)
    high_slot = jax.random.randint(second_key, (), 0, N_HEAD)
    slots = jnp.arange(N_HEAD)
    values = jnp.where(slots == high_slot, highest, values)
    return values.astype(jnp.int32)


def touch_ends(values, stream_key, low, top_value):
    extent = values.shape
    place = [jax.random.randint(jax.random.fold_in(stream_key, axis), (), 0, extent[axis]) for axis in range(len(extent))]
    values = values.at[tuple(place)].set(low)
    longest = extent.index(max(extent))
    place[longest] = (place[longest] + 1) % extent[longest]
    return values.at[tuple(place)].set(top_value)


def setup_inputs(seed: int = 0) -> dict:
    arg_keys = jax.random.split(jax.random.key(seed), 6)
    queries = draw_queries(jax.random.fold_in(arg_keys[5], 71), 0)
    keys = draw_keys(jax.random.fold_in(arg_keys[5], 71), 0)
    head_pick = touch_ends(jax.random.randint(arg_keys[2], (N_HEAD,), 0, QH), jax.random.fold_in(arg_keys[2], 1), 0, QH - 1).astype(jnp.int32)
    block_offset = draw_block_offset(jax.random.fold_in(arg_keys[5], 71), 0)
    owner_map = jax.random.permutation(arg_keys[4], KBLK).astype(jnp.int32)
    return {"queries": queries, "keys": keys, "head_pick": head_pick, "block_offset": block_offset, "owner_map": owner_map}


def reference(queries, keys, head_pick, block_offset, owner_map):
    row_block = math.gcd(QUERIES, 512)
    scale = HD ** -0.5
    key_positions = jnp.arange(KEYS, dtype=jnp.int32)

    def one_head(entry):
        head_queries, pick, offset = entry
        chosen = lax.dynamic_index_in_dim(keys, pick // (QH // KV), 0, keepdims=False)
        grouped = head_queries.reshape(QUERIES // row_block, row_block, HD)

        def one_block(block_entry):
            number, rows = block_entry
            query_positions = offset * BLK + number * row_block + jnp.arange(row_block, dtype=jnp.int32)
            scores = jnp.dot(rows, chosen.T, preferred_element_type=jnp.float32) * scale
            allowed = key_positions[None, :] <= query_positions[:, None]
            masked = jnp.where(allowed, scores, -1.0e30)
            row_top = jnp.max(masked, axis=1, keepdims=True)
            weights = jnp.where(allowed, jnp.exp(masked - row_top), 0.0)
            prob = weights / jnp.sum(weights, axis=1, keepdims=True)
            per_key = prob.reshape(row_block, KBLK, BLK).sum(axis=2)
            return per_key.reshape(row_block // BLK, BLK, KBLK).sum(axis=1)

        mass = lax.map(one_block, (jnp.arange(QUERIES // row_block, dtype=jnp.int32), grouped))
        mass = mass.reshape(QBLK, KBLK)
        return jnp.take(mass.T, owner_map, axis=0)

    return lax.map(one_head, (queries, head_pick, block_offset))
```

```python
import functools

import jax
import jax.numpy as jnp
from jax import lax
from jax.experimental import pallas as pl
from jax.experimental.pallas import tpu as pltpu
from jax.sharding import PartitionSpec as P

QH = 64
KV = 8
HD = 128
BLK = 128
NH = 8
NZ = 16
PLANE = 4
Q_DEV = 256
K_DEV = 384
PIECE = K_DEV // NH
KBD = K_DEV // BLK
PKB = PLANE * KBD
HALF = NZ // 2
NEGATIVE = -1e30
SCALE2 = 1.4426950408889634 * HD**-0.5
MESH = pl.DeviceIdType.MESH


def kernel(
    q_ref, k_ref, pick_ref, off_ref, own_ref, o_ref,
    qall, kp, stage1, recv1, stage2, table, probs, maxes, stats, stat_in, reply_out, reply_in,
    mass_out, mass_in, picked, lanes, plane_out, plane_in,
    ring_send, ring_recv, s1_send, s1_recv, s2_send, s2_recv, s3_send, s3_recv,
    st_send, st_recv, rp_send, rp_recv, ms_send, ms_recv, pe_send, pe_recv,
):
    head = lax.axis_index("head")
    seq = lax.axis_index("seq")
    z = seq // PLANE
    cls = seq % PLANE
    xl = cls // 2
    core = cls % 2

    def at_z(other):
        return {"head": head, "seq": lax.rem(other + NZ, NZ) * PLANE + cls}

    def remote(src, dst, send, recv, device):
        return pltpu.make_async_remote_copy(
            src_ref=src, dst_ref=dst, send_sem=send, recv_sem=recv,
            device_id=device, device_id_type=MESH,
        )

    barrier = pltpu.get_barrier_semaphore()
    peers = 0
    for step in range(1, NZ):
        pl.semaphore_signal(barrier, inc=1, device_id=at_z(z + step), device_id_type=MESH)
        peers += 1
    for gi in range(NH):
        for xo in range(2):
            if gi or xo:
                target = {"head": lax.rem(head + gi, NH), "seq": z * PLANE + lax.rem(xl + xo, 2) * 2 + core}
                pl.semaphore_signal(barrier, inc=1, device_id=target, device_id_type=MESH)
                peers += 1
    for xo in range(2):
        target = {"head": head, "seq": z * PLANE + lax.rem(xl + xo, 2) * 2 + (1 - core)}
        pl.semaphore_signal(barrier, inc=1, device_id=target, device_id_type=MESH)
        peers += 1

    qall[z] = q_ref[...]
    picks = jnp.full((16, HD), (pick_ref[0] // (QH // KV)).astype(jnp.float32), jnp.float32).astype(jnp.bfloat16)
    for m in range(NH):
        stage1[m, 0:PIECE, :] = k_ref[m * PIECE:(m + 1) * PIECE, :]
        stage1[m, PIECE:PIECE + 16, :] = picks
    recv1[head] = stage1[head]
    key_local = lax.broadcasted_iota(jnp.int32, (BLK, BLK), 0)
    query_local = lax.broadcasted_iota(jnp.int32, (BLK, BLK), 1)
    table[0] = jnp.full((BLK, BLK), NEGATIVE, jnp.float32)
    table[1] = jnp.where(key_local <= query_local, 0.0, NEGATIVE)
    table[2] = jnp.zeros((BLK, BLK), jnp.float32)
    probs[...] = jnp.zeros_like(probs)
    stats[...] = jnp.zeros_like(stats)

    pl.semaphore_wait(barrier, peers)

    def ring_copy(direction, d):
        sign = 1 if direction == 0 else -1
        slot = lax.rem(z - sign * (d - 1) + NZ, NZ)
        if d == HALF:
            rows = pl.ds(direction * BLK, BLK)
            ref = qall.at[slot, rows, :]
        else:
            ref = qall.at[slot]
        return remote(
            ref, ref, ring_send.at[direction, d - 1], ring_recv.at[direction, d - 1], at_z(z + sign)
        )

    def ring_arrival(direction, d):
        sign = 1 if direction == 0 else -1
        slot = lax.rem(z - sign * d + NZ, NZ)
        if d == HALF:
            ref = qall.at[slot, pl.ds(direction * BLK, BLK), :]
        else:
            ref = qall.at[slot]
        return remote(
            ref, ref, ring_send.at[direction, d - 1], ring_recv.at[direction, d - 1], at_z(z + sign)
        )

    def ring_step(d):
        for direction in range(2):
            ring_arrival(direction, d).wait_recv()
            if d < HALF:
                ring_copy(direction, d + 1).start()

    def s1_copy(i):
        other = lax.rem(head + i, NH)
        return remote(
            stage1.at[other], recv1.at[head], s1_send.at[i], s1_recv.at[i], {"head": other, "seq": seq}
        )

    def s1_arrival(i):
        other = lax.rem(head - i + NH, NH)
        return remote(
            stage1.at[other], recv1.at[other], s1_send.at[i], s1_recv.at[i], {"head": other, "seq": seq}
        )

    def s2_copy(gi, xo):
        other = lax.rem(head + gi, NH)
        target = {"head": other, "seq": z * PLANE + lax.rem(xl + xo, 2) * 2 + core}
        return remote(
            stage2.at[other], kp.at[pl.ds(cls * K_DEV + head * PIECE, PIECE), :],
            s2_send.at[gi, xo], s2_recv.at[gi, xo], target,
        )

    def s2_arrival(gi, xo):
        other = lax.rem(head - gi + NH, NH)
        ox = lax.rem(xl + xo, 2)
        source = {"head": other, "seq": z * PLANE + ox * 2 + core}
        return remote(
            stage2.at[other], kp.at[pl.ds((ox * 2 + core) * K_DEV + other * PIECE, PIECE), :],
            s2_send.at[gi, xo], s2_recv.at[gi, xo], source,
        )

    partner = {"head": head, "seq": z * PLANE + xl * 2 + (1 - core)}

    def s3_copy(xo, c):
        ref = kp.at[pl.ds((2 * xo + c) * K_DEV, K_DEV), :]
        return remote(ref, ref, s3_send.at[xo], s3_recv.at[xo], partner)

    for direction in range(2):
        ring_copy(direction, 1).start()
    for i in range(1, NH):
        s1_copy(i).start()
    ring_step(1)
    for i in range(1, NH):
        s1_arrival(i).wait_recv()
    pieces = [recv1[m, 0:PIECE, :].astype(jnp.float32) for m in range(NH)]
    for g in range(NH):
        wanted = recv1[g, PIECE:PIECE + 16, :].astype(jnp.float32)[0:8]
        wanted = jnp.concatenate([wanted] * (PIECE // 8), axis=0)
        chosen = pieces[0]
        for m in range(1, NH):
            chosen = jnp.where(wanted == float(m), pieces[m], chosen)
        stage2[g] = chosen.astype(jnp.bfloat16)
    kp[pl.ds(cls * K_DEV + head * PIECE, PIECE), :] = stage2[head]
    s2_pairs = [(gi, xo) for gi in range(NH) for xo in range(2) if gi or xo]
    for gi, xo in s2_pairs:
        s2_copy(gi, xo).start()
    ring_step(2)
    for gi, xo in s2_pairs:
        s2_arrival(gi, xo).wait_recv()
    for xo in range(2):
        s3_copy(xo, core).start()
    ring_step(3)
    for xo in range(2):
        s3_copy(xo, 1 - core).wait_recv()

    offset = off_ref[0]

    def compute(item, unused):
        d = (item + 1) // 2
        down = 1 - lax.rem(item, 2)
        signed = jnp.where(down == 1, d, -d)
        slot = lax.rem(z + signed + NZ, NZ)
        q = qall[slot]
        blocks = [[], []]
        for kb in range(PKB):
            s = lax.dot_general(
                kp[kb * BLK:(kb + 1) * BLK, :], q, (((1,), (1,)), ((), ())),
                preferred_element_type=jnp.float32,
            )
            for j in range(2):
                ahead = slot * 8 + cls * 2 + j + offset - (z * PKB + kb)
                which = jnp.clip(ahead + 1, 0, 2)
                sj = s[:, j * BLK:(j + 1) * BLK] + table[which]
                top = jnp.max(sj, axis=0, keepdims=True)
                total = jnp.sum(jnp.exp2((sj - top) * SCALE2), axis=0, keepdims=True)
                row = 4 * (kb // KBD) + kb % KBD
                maxes[j, row:row + 1, :] = top
                probs[slot, j, row:row + 1, :] = total
        for j in range(2):
            tops = maxes[j]
            used = lax.rem(lax.broadcasted_iota(jnp.int32, (16, BLK), 0), 4) < KBD
            tops = jnp.where(used, tops, NEGATIVE)
            top = jnp.max(tops, axis=0, keepdims=True)
            scaled = jnp.where(used, probs[slot, j] * jnp.exp2((tops - top) * SCALE2), 0.0)
            probs[slot, j] = scaled
            stats[slot, 2 * j:2 * j + 1, :] = top
            stats[slot, 2 * j + 1:2 * j + 2, :] = jnp.sum(scaled, axis=0, keepdims=True)
        return unused

    def st_copy(r):
        slot = lax.rem(z + HALF + r, NZ)
        return remote(stats.at[slot], stat_in.at[z], st_send.at[r], st_recv.at[r], at_z(z + r))

    def st_arrival(r):
        source = lax.rem(z - r + NZ, NZ)
        return remote(stats.at[source], stat_in.at[source], st_send.at[r], st_recv.at[r], at_z(z + r))

    def send_stats(lo, hi):
        for item in range(lo, hi):
            d = (item + 1) // 2
            r = HALF - d if item % 2 == 1 or item == 0 else HALF + d
            st_copy(r).start()

    def run(lo, hi):
        lax.fori_loop(lo, hi, compute, 0)
        send_stats(lo, min(hi, 2 * HALF - 1))

    run(0, 3)
    ring_step(4)
    run(3, 7)
    ring_step(5)
    run(7, 10)
    ring_step(6)
    run(10, 13)
    ring_step(7)
    run(13, 15)
    ring_step(8)
    lax.fori_loop(15, 16, compute, 0)

    far = lax.rem(z + HALF, NZ)
    stat_in[z] = stats[far]
    for r in range(1, NZ):
        st_arrival(r).wait_recv()
    out_rows = []
    for j in range(2):
        tops = stat_in[:, 2 * j, :]
        top = jnp.max(tops, axis=0, keepdims=True)
        total = jnp.sum(stat_in[:, 2 * j + 1, :] * jnp.exp2((tops - top) * SCALE2), axis=0, keepdims=True)
        reply_out[2 * j:2 * j + 1, :] = top
        reply_out[2 * j + 1:2 * j + 2, :] = 1.0 / total
    reply_out[4:8, :] = jnp.zeros((4, BLK), jnp.float32)
    reply_in[far] = reply_out[...]

    def rp_copy(r):
        return remote(reply_out, reply_in.at[far], rp_send.at[r], rp_recv.at[r], at_z(z + r))

    def rp_arrival(r):
        slot = lax.rem(z - r + HALF + NZ, NZ)
        return remote(reply_out, reply_in.at[slot], rp_send.at[r], rp_recv.at[r], at_z(z + r))

    for r in range(1, NZ):
        rp_copy(r).start()

    lane = lax.broadcasted_iota(jnp.int32, (16, BLK), 1)
    mass = jnp.zeros((16, BLK), jnp.float32)
    order = [0]
    for d in range(1, HALF):
        order += [d, NZ - d]
    order.append(HALF)
    for r in order:
        if r:
            rp_arrival(r).wait_recv()
        slot = lax.rem(z - r + HALF + NZ, NZ)
        for j in range(2):
            top = reply_in[slot, 2 * j:2 * j + 1, :]
            weight = jnp.exp2((stats[slot, 2 * j:2 * j + 1, :] - top) * SCALE2) * reply_in[slot, 2 * j + 1:2 * j + 2, :]
            column = jnp.sum(probs[slot, j] * weight, axis=1, keepdims=True)
            mass = jnp.where(lane == slot * 2 + j, column, mass)
    packed = mass[0:4]
    for part in range(1, 4):
        packed = packed + pltpu.roll(mass[4 * part:4 * part + 4], 32 * part, 1)
    mass_out[...] = packed
    mass_in[z] = packed

    def ms_copy(r):
        return remote(mass_out, mass_in.at[z], ms_send.at[r], ms_recv.at[r], at_z(z + r))

    def ms_arrival(r):
        source = lax.rem(z - r + NZ, NZ)
        return remote(mass_out, mass_in.at[source], ms_send.at[r], ms_recv.at[r], at_z(z + r))

    for r in range(1, NZ):
        ms_copy(r).start()
    for c in range(PLANE):
        for t in range(KBD):
            block = own_ref[z * PKB + c * KBD + t]
            lanes[4 * c + t:4 * c + t + 1, :] = jnp.full((1, BLK), 32 * (lax.rem(block, PKB) // KBD), jnp.int32)
        lanes[4 * c + 3:4 * c + 4, :] = jnp.zeros((1, BLK), jnp.int32)
        picked[4 * c + 3:4 * c + 4, :] = jnp.zeros((1, BLK), jnp.float32)
    for r in range(1, NZ):
        ms_arrival(r).wait_recv()
    for c in range(PLANE):
        for t in range(KBD):
            block = own_ref[z * PKB + c * KBD + t]
            picked[4 * c + t:4 * c + t + 1, :] = mass_in[block // PKB, pl.ds(lax.rem(block, KBD), 1), :]
    where_from = lanes[...] + lane // 8 * 2 + lane % 2
    spread = jnp.take_along_axis(picked[...], where_from, axis=1)
    spread = jnp.where(lane // 2 % 4 == cls, spread, 0.0)
    for c in range(PLANE):
        plane_out[c] = spread[4 * c:4 * c + 4]
    plane_in[cls] = plane_out[cls]

    def pe_copy(i):
        other = lax.rem(cls + i, PLANE)
        return remote(
            plane_out.at[other], plane_in.at[cls], pe_send.at[i], pe_recv.at[i],
            {"head": head, "seq": z * PLANE + other},
        )

    def pe_arrival(i):
        other = lax.rem(cls - i + PLANE, PLANE)
        return remote(
            plane_out.at[other], plane_in.at[other], pe_send.at[i], pe_recv.at[i],
            {"head": head, "seq": z * PLANE + other},
        )

    for i in range(1, PLANE):
        pe_copy(i).start()
    for i in range(1, PLANE):
        pe_arrival(i).wait_recv()
    final = plane_in[0] + plane_in[1] + plane_in[2] + plane_in[3]
    o_ref[0] = final[0:KBD]

    for direction in range(2):
        for d in range(1, HALF + 1):
            ring_copy(direction, d).wait_send()
    for i in range(1, NH):
        s1_copy(i).wait_send()
    for gi, xo in s2_pairs:
        s2_copy(gi, xo).wait_send()
    for xo in range(2):
        s3_copy(xo, core).wait_send()
    for r in range(1, NZ):
        st_copy(r).wait_send()
        rp_copy(r).wait_send()
        ms_copy(r).wait_send()
    for i in range(1, PLANE):
        pe_copy(i).wait_send()


def body(queries, keys, head_pick, block_offset, owner_map):
    vmem = pl.BlockSpec(memory_space=pltpu.VMEM)
    smem = pl.BlockSpec(memory_space=pltpu.SMEM)
    f32, bf16 = jnp.float32, jnp.bfloat16
    dma = pltpu.SemaphoreType.DMA
    return pl.pallas_call(
        kernel,
        out_shape=jax.ShapeDtypeStruct((1, KBD, BLK), f32),
        in_specs=[vmem, vmem, smem, smem, smem],
        out_specs=vmem,
        scratch_shapes=[
            pltpu.VMEM((NZ, Q_DEV, HD), bf16),
            pltpu.VMEM((PLANE * K_DEV, HD), bf16),
            pltpu.VMEM((NH, PIECE + 16, HD), bf16),
            pltpu.VMEM((NH, PIECE + 16, HD), bf16),
            pltpu.VMEM((NH, PIECE, HD), bf16),
            pltpu.VMEM((3, BLK, BLK), f32),
            pltpu.VMEM((NZ, 2, 16, BLK), f32),
            pltpu.VMEM((2, 16, BLK), f32),
            pltpu.VMEM((NZ, 8, BLK), f32),
            pltpu.VMEM((NZ, 8, BLK), f32),
            pltpu.VMEM((8, BLK), f32),
            pltpu.VMEM((NZ, 8, BLK), f32),
            pltpu.VMEM((4, BLK), f32),
            pltpu.VMEM((NZ, 4, BLK), f32),
            pltpu.VMEM((16, BLK), f32),
            pltpu.VMEM((16, BLK), jnp.int32),
            pltpu.VMEM((PLANE, 4, BLK), f32),
            pltpu.VMEM((PLANE, 4, BLK), f32),
            dma((2, HALF)), dma((2, HALF)),
            dma((NH,)), dma((NH,)),
            dma((NH, 2)), dma((NH, 2)),
            dma((2,)), dma((2,)),
            dma((NZ,)), dma((NZ,)),
            dma((NZ,)), dma((NZ,)),
            dma((NZ,)), dma((NZ,)),
            dma((PLANE,)), dma((PLANE,)),
        ],
        compiler_params=pltpu.CompilerParams(
            collective_id=0, has_side_effects=True, vmem_limit_bytes=32 * 1024 * 1024
        ),
        cost_estimate=pl.CostEstimate(flops=1610612736, bytes_accessed=165000, transcendentals=6291456),
    )(queries[0], keys[0], head_pick, block_offset, owner_map)


def solution(mesh):
    return jax.shard_map(
        body,
        mesh=mesh,
        in_specs=(P("head", "seq", None), P("head", "seq", None), P("head"), P("head"), P()),
        out_specs=P("head", "seq", None),
        check_vma=False,
    )
```

```python
import jax
import jax.numpy as jnp
from jax import lax
from jax.experimental import pallas as pl
from jax.experimental.pallas import tpu as pltpu
from jax.sharding import PartitionSpec as P

QH = 64
KV = 8
HD = 128
BLK = 128
NH = 8
NZ = 16
PLANE = 4
Q_DEV = 256
K_DEV = 384
PIECE = K_DEV // NH
KBD = K_DEV // BLK
PKB = PLANE * KBD
ROWS = 2 * PKB
HALF = NZ // 2
CHUNKS = 4
CHUNK = Q_DEV // CHUNKS
FIRST = 5
NEGATIVE = -1e30
SCALE2 = 1.4426950408889634 * HD**-0.5
MESH = pl.DeviceIdType.MESH


def kernel(
    q_ref, k_ref, pick_ref, off_ref, own_ref, o_ref,
    qall, kp, pick_out, picks, recv1, stage2, table, probs, tops, maxes, prob_in, top_in, weighted,
    mass_out, mass_in, plane_out, plane_in,
    local_sem, greet, ring_send, ring_recv, pk_send, pk_recv, s1_send, s1_recv, s2_send, s2_recv, s3_send, s3_recv,
    pr_send, pr_recv, tp_send, tp_recv, ms_send, ms_recv, pe_send, pe_recv,
):
    head = lax.axis_index("head")
    seq = lax.axis_index("seq")
    z = seq // PLANE
    cls = seq % PLANE
    xl = cls // 2
    core = cls % 2

    def wrap(other):
        return lax.rem(other + NZ, NZ)

    def at_z(other):
        return {"head": head, "seq": wrap(other) * PLANE + cls}

    def at_head(i):
        return {"head": lax.rem(head + i + NH, NH), "seq": seq}

    def at_pair(gi, xo):
        return {"head": lax.rem(head + gi + NH, NH), "seq": z * PLANE + lax.rem(xl + xo, 2) * 2 + core}

    def at_plane(c):
        return {"head": head, "seq": z * PLANE + lax.rem(c + PLANE, PLANE)}

    def remote(src, dst, send, recv, device):
        return pltpu.make_async_remote_copy(
            src_ref=src, dst_ref=dst, send_sem=send, recv_sem=recv,
            device_id=device, device_id_type=MESH,
        )

    def signal(sem, device):
        pl.semaphore_signal(sem, inc=1, device_id=device, device_id_type=MESH)

    barrier = pltpu.get_barrier_semaphore()
    s2_pairs = [(gi, xo) for gi in range(NH) for xo in range(2) if gi or xo]
    near = [at_z(z + 1), at_z(z - 1)]
    near += [at_pair(gi, xo) for gi, xo in s2_pairs]
    near += [{"head": head, "seq": z * PLANE + lax.rem(xl + xo, 2) * 2 + (1 - core)} for xo in range(2)]
    for device in near:
        signal(barrier, device)

    own_q = pltpu.make_async_copy(q_ref, qall.at[z], local_sem.at[0])
    own_k = pltpu.make_async_copy(k_ref.at[pl.ds(head * PIECE, PIECE), :], recv1.at[head], local_sem.at[1])
    own_q.start()
    own_k.start()
    picked = (pick_ref[0] // (QH // KV)).astype(jnp.float32)
    pick_out[...] = jnp.full((16, HD), picked, jnp.float32).astype(jnp.bfloat16)
    picks[head] = pick_out[...]

    pl.semaphore_wait(barrier, len(near))

    def ring_copy(direction, d, c, src=None):
        sign = 1 - 2 * direction
        ref = qall.at[wrap(z - sign * (d - 1)), pl.ds(c * CHUNK, CHUNK), :]
        return remote(
            ref if src is None else src, ref,
            ring_send.at[direction, d - 1, c], ring_recv.at[direction, d - 1, c], at_z(z + sign),
        )

    def ring_arrival(direction, d, c):
        sign = 1 - 2 * direction
        ref = qall.at[wrap(z - sign * d), pl.ds(c * CHUNK, CHUNK), :]
        return remote(
            ref, ref, ring_send.at[direction, d - 1, c], ring_recv.at[direction, d - 1, c], at_z(z + sign)
        )

    def first_ring_copy(direction, c):
        return ring_copy(direction, 1, c, q_ref.at[pl.ds(c * CHUNK, CHUNK), :])

    def serve(d, c):
        for direction in range(2):
            ring_arrival(direction, d, c).wait_recv()
            if isinstance(d, int):
                ring_copy(direction, d + 1, c).start()
            else:
                mine = c < CHUNKS // 2 if direction == 0 else c >= CHUNKS // 2

                @pl.when(jnp.logical_or(d < HALF - 1, mine))
                def _():
                    ring_copy(direction, d + 1, c).start()

    def ring_step(d):
        for c in range(CHUNKS):
            serve(d, c)

    def s1_copy(i):
        other = lax.rem(head + i, NH)
        return remote(
            k_ref.at[pl.ds(other * PIECE, PIECE), :], recv1.at[head], s1_send.at[i], s1_recv.at[i], at_head(i)
        )

    def s1_arrival(i):
        other = lax.rem(head - i + NH, NH)
        return remote(
            k_ref.at[pl.ds(other * PIECE, PIECE), :], recv1.at[other], s1_send.at[i], s1_recv.at[i], at_head(-i)
        )

    def pk_copy(i):
        return remote(pick_out, picks.at[head], pk_send.at[i], pk_recv.at[i], at_head(i))

    def pk_arrival(i):
        other = lax.rem(head - i + NH, NH)
        return remote(pick_out, picks.at[other], pk_send.at[i], pk_recv.at[i], at_head(-i))

    def s2_copy(gi, xo):
        other = lax.rem(head + gi, NH)
        return remote(
            stage2.at[other], kp.at[pl.ds(cls * K_DEV + head * PIECE, PIECE), :],
            s2_send.at[gi, xo], s2_recv.at[gi, xo], at_pair(gi, xo),
        )

    def s2_arrival(gi, xo):
        other = lax.rem(head - gi + NH, NH)
        start = (lax.rem(xl + xo, 2) * 2 + core) * K_DEV + other * PIECE
        return remote(
            stage2.at[other], kp.at[pl.ds(start, PIECE), :],
            s2_send.at[gi, xo], s2_recv.at[gi, xo], at_pair(-gi, xo),
        )

    def s3_copy(xo, c):
        ref = kp.at[pl.ds((2 * xo + c) * K_DEV, K_DEV), :]
        return remote(
            ref, ref, s3_send.at[xo], s3_recv.at[xo], {"head": head, "seq": z * PLANE + xl * 2 + (1 - core)}
        )

    for i in range(1, NH):
        pk_copy(i).start()
    for c in range(CHUNKS):
        for direction in range(2):
            first_ring_copy(direction, c).start()
    for i in range(1, NH):
        s1_copy(i).start()
    for side in range(2):
        signal(greet.at[0, side], at_z(z + 1 - 2 * side))

    key_local = lax.broadcasted_iota(jnp.int32, (BLK, BLK), 0)
    query_local = lax.broadcasted_iota(jnp.int32, (BLK, BLK), 1)
    table[0] = jnp.full((BLK, BLK), NEGATIVE, jnp.float32)
    table[1] = jnp.where(key_local <= query_local, 0.0, NEGATIVE)
    table[2] = jnp.zeros((BLK, BLK), jnp.float32)

    ring_step(1)
    for side in range(2):
        pl.semaphore_wait(greet.at[0, side], 1)
    for side in range(2):
        signal(greet.at[1, side], at_z(z + 2 - 4 * side))
    own_k.wait()
    for i in range(1, NH):
        pk_arrival(i).wait_recv()
        s1_arrival(i).wait_recv()
    pieces = [recv1[m].astype(jnp.float32) for m in range(NH)]
    for g in range(NH):
        wanted = picks[g].astype(jnp.float32)[0:8]
        wanted = jnp.concatenate([wanted] * (PIECE // 8), axis=0)
        chosen = pieces[0]
        for m in range(1, NH):
            chosen = jnp.where(wanted == float(m), pieces[m], chosen)
        stage2[g] = chosen.astype(jnp.bfloat16)
    for gi, xo in s2_pairs:
        s2_copy(gi, xo).start()
    kp[pl.ds(cls * K_DEV + head * PIECE, PIECE), :] = stage2[head]
    ring_step(2)
    for side in range(2):
        pl.semaphore_wait(greet.at[1, side], 1)
    for side in range(2):
        signal(greet.at[2, side], at_z(z + 4 - 8 * side))
    ring_step(3)
    for gi, xo in s2_pairs:
        s2_arrival(gi, xo).wait_recv()
    for xo in range(2):
        s3_copy(xo, core).start()
    ring_step(4)
    for side in range(2):
        pl.semaphore_wait(greet.at[2, side], 1)
    for xo in range(2):
        s3_copy(xo, 1 - core).wait_recv()
    own_q.wait()

    offset = off_ref[0]
    far = wrap(z + HALF)

    def pr_copy(r):
        return remote(probs.at[wrap(z + HALF + r)], prob_in.at[z], pr_send.at[r], pr_recv.at[r], at_z(z + r))

    def tp_copy(r):
        return remote(tops.at[wrap(z + HALF + r)], top_in.at[z], tp_send.at[r], tp_recv.at[r], at_z(z + r))

    def pr_arrival(r):
        source = wrap(z - r)
        return remote(probs.at[source], prob_in.at[source], pr_send.at[r], pr_recv.at[r], at_z(z - r))

    def tp_arrival(r):
        source = wrap(z - r)
        return remote(tops.at[source], top_in.at[source], tp_send.at[r], tp_recv.at[r], at_z(z - r))

    def compute(item, unused):
        later = HALF * 2 - CHUNKS

        @pl.when(item < later)
        def _():
            serve(FIRST + item // CHUNKS, lax.rem(item, CHUNKS))

        @pl.when(item == 2 * HALF - 1)
        def _():
            for c in range(CHUNKS):
                ring_arrival(2 * c // CHUNKS, HALF, c).wait_recv()

        d = (item + 1) // 2
        signed = jnp.where(lax.rem(item, 2) == 1, -d, d)
        slot = wrap(z + signed)
        q = qall[slot]
        for kb in range(PKB):
            s = lax.dot_general(
                kp[kb * BLK:(kb + 1) * BLK, :], q, (((1,), (1,)), ((), ())),
                preferred_element_type=jnp.float32,
            )
            for j in range(2):
                ahead = slot * 8 + cls * 2 + j + offset - (z * PKB + kb)
                sj = s[:, j * BLK:(j + 1) * BLK] + table[jnp.clip(ahead + 1, 0, 2)]
                top = jnp.max(sj, axis=0, keepdims=True)
                row = j * PKB + kb
                maxes[row:row + 1, :] = top
                probs[slot, row:row + 1, :] = jnp.sum(jnp.exp2((sj - top) * SCALE2), axis=0, keepdims=True)
        first = lax.broadcasted_iota(jnp.int32, (ROWS, BLK), 0) < PKB
        every = maxes[...]
        top0 = jnp.max(jnp.where(first, every, NEGATIVE), axis=0, keepdims=True)
        top1 = jnp.max(jnp.where(first, NEGATIVE, every), axis=0, keepdims=True)
        tops[slot, 0:1, :] = top0
        tops[slot, 1:2, :] = top1
        probs[slot] = probs[slot] * jnp.exp2((every - jnp.where(first, top0, top1)) * SCALE2)
        r = HALF + signed

        @pl.when(item < 2 * HALF - 1)
        def _():
            pr_copy(r).start()
            tp_copy(r).start()

        return unused

    lax.fori_loop(0, 2 * HALF, compute, 0)

    prob_in[z] = probs[far]
    top_in[z] = tops[far]
    for direction in range(2):
        for d in range(1, HALF):
            for c in range(CHUNKS):
                (first_ring_copy(direction, c) if d == 1 else ring_copy(direction, d, c)).wait_send()
    for i in range(1, NH):
        pk_copy(i).wait_send()
        s1_copy(i).wait_send()
    for gi, xo in s2_pairs:
        s2_copy(gi, xo).wait_send()
    for xo in range(2):
        s3_copy(xo, core).wait_send()
    for r in range(1, NZ):
        tp_arrival(r).wait_recv()
        pr_arrival(r).wait_recv()
    each = top_in[...]
    top = jnp.max(each, axis=0, keepdims=True)
    factor = jnp.exp2((each - top) * SCALE2)
    first = lax.broadcasted_iota(jnp.int32, (ROWS, BLK), 0) < PKB
    total = jnp.zeros((ROWS, BLK), jnp.float32)
    for source in range(NZ):
        part = prob_in[source] * jnp.where(first, factor[source, 0:1], factor[source, 1:2])
        total = total + part
        weighted[source * ROWS:(source + 1) * ROWS, :] = part
    sum0 = jnp.sum(jnp.where(first, total, 0.0), axis=0, keepdims=True)
    sum1 = jnp.sum(jnp.where(first, 0.0, total), axis=0, keepdims=True)
    inverse = 1.0 / jnp.where(lax.broadcasted_iota(jnp.int32, (8, BLK), 0) == 0, sum0, sum1)
    mass = lax.dot_general(
        inverse, weighted[...], (((1,), (1,)), ((), ())),
        precision=lax.Precision.HIGHEST, preferred_element_type=jnp.float32,
    )
    column = lax.broadcasted_iota(jnp.int32, (1, NZ * ROWS), 1)
    mass_out[...] = jnp.where(lax.rem(column, ROWS) < PKB, mass[0:1], mass[1:2])
    mass_in[far] = mass_out[...]

    def ms_copy(r):
        return remote(mass_out, mass_in.at[far], ms_send.at[r], ms_recv.at[r], at_z(z + r))

    def ms_arrival(r):
        source = wrap(z - r + HALF)
        return remote(mass_out, mass_in.at[source], ms_send.at[r], ms_recv.at[r], at_z(z - r))

    for d in range(HALF):
        ms_copy(HALF - d).start()
        if d:
            ms_copy(HALF + d).start()
    wide = lax.broadcasted_iota(jnp.int32, (8, NZ * ROWS), 1)
    sub = lax.broadcasted_iota(jnp.int32, (8, NZ * ROWS), 0)
    chosen = []
    for j in range(2):
        for c in range(0, PLANE, 2):
            place = jnp.full((8, NZ * ROWS), -1, jnp.int32)
            for row in range(8):
                if row % 4 < KBD:
                    block = own_ref[z * PKB + (c + row // 4) * KBD + row % 4]
                    lane = block // PKB * ROWS + j * PKB + lax.rem(block, PKB)
                    place = jnp.where(sub == row, lane, place)
            chosen.append(jnp.where(wide == place, 1.0, 0.0))
    chosen = jnp.concatenate(chosen, axis=0)
    for r in range(1, NZ):
        pr_copy(r).wait_send()
        tp_copy(r).wait_send()
    for c in range(CHUNKS):
        ring_copy(2 * c // CHUNKS, HALF, c).wait_send()
    for r in range(1, NZ):
        ms_arrival(r).wait_recv()
    spread = jnp.concatenate(
        [jnp.where(sub == 0, jnp.broadcast_to(mass_in[piece], (8, NZ * ROWS)), 0.0) for piece in range(NZ)], axis=0
    )
    rows = lax.dot_general(
        chosen, spread, (((1,), (1,)), ((), ())),
        precision=lax.Precision.HIGHEST, preferred_element_type=jnp.float32,
    )
    rows = pltpu.roll(rows[0:16] + pltpu.roll(rows[16:32], 1, 1), 2 * cls, 1)
    for c in range(PLANE):
        plane_out[c] = rows[4 * c:4 * c + 4]
    plane_in[cls] = plane_out[cls]

    def pe_copy(i):
        other = lax.rem(cls + i, PLANE)
        return remote(plane_out.at[other], plane_in.at[cls], pe_send.at[i], pe_recv.at[i], at_plane(cls + i))

    def pe_arrival(i):
        other = lax.rem(cls - i + PLANE, PLANE)
        return remote(plane_out.at[other], plane_in.at[other], pe_send.at[i], pe_recv.at[i], at_plane(cls - i))

    for i in range(1, PLANE):
        pe_copy(i).start()
    for r in range(1, NZ):
        ms_copy(r).wait_send()
    for i in range(1, PLANE):
        pe_arrival(i).wait_recv()
    final = plane_in[0] + plane_in[1] + plane_in[2] + plane_in[3]
    o_ref[0] = final[0:KBD]
    for i in range(1, PLANE):
        pe_copy(i).wait_send()


def body(queries, keys, head_pick, block_offset, owner_map):
    vmem = pl.BlockSpec(memory_space=pltpu.VMEM)
    smem = pl.BlockSpec(memory_space=pltpu.SMEM)
    hbm = pl.BlockSpec(memory_space=pl.ANY)
    f32, bf16 = jnp.float32, jnp.bfloat16
    dma = pltpu.SemaphoreType.DMA
    return pl.pallas_call(
        kernel,
        out_shape=jax.ShapeDtypeStruct((1, KBD, BLK), f32),
        in_specs=[hbm, hbm, smem, smem, smem],
        out_specs=vmem,
        scratch_shapes=[
            pltpu.VMEM((NZ, Q_DEV, HD), bf16),
            pltpu.VMEM((PLANE * K_DEV, HD), bf16),
            pltpu.VMEM((16, HD), bf16),
            pltpu.VMEM((NH, 16, HD), bf16),
            pltpu.VMEM((NH, PIECE, HD), bf16),
            pltpu.VMEM((NH, PIECE, HD), bf16),
            pltpu.VMEM((3, BLK, BLK), f32),
            pltpu.VMEM((NZ, ROWS, BLK), f32),
            pltpu.VMEM((NZ, 2, BLK), f32),
            pltpu.VMEM((ROWS, BLK), f32),
            pltpu.VMEM((NZ, ROWS, BLK), f32),
            pltpu.VMEM((NZ, 2, BLK), f32),
            pltpu.VMEM((NZ * ROWS, BLK), f32),
            pltpu.VMEM((1, NZ * ROWS), f32),
            pltpu.VMEM((NZ, 1, NZ * ROWS), f32),
            pltpu.VMEM((PLANE, 4, BLK), f32),
            pltpu.VMEM((PLANE, 4, BLK), f32),
            dma((2,)), pltpu.SemaphoreType.REGULAR((3, 2)),
            dma((2, HALF, CHUNKS)), dma((2, HALF, CHUNKS)),
            dma((NH,)), dma((NH,)),
            dma((NH,)), dma((NH,)),
            dma((NH, 2)), dma((NH, 2)),
            dma((2,)), dma((2,)),
            dma((NZ,)), dma((NZ,)),
            dma((NZ,)), dma((NZ,)),
            dma((NZ,)), dma((NZ,)),
            dma((PLANE,)), dma((PLANE,)),
        ],
        compiler_params=pltpu.CompilerParams(
            collective_id=0, has_side_effects=True, vmem_limit_bytes=60 * 1024 * 1024
        ),
        cost_estimate=pl.CostEstimate(flops=1610612736, bytes_accessed=165000, transcendentals=6291456),
    )(queries[0], keys[0], head_pick, block_offset, owner_map)


def solution(mesh):
    return jax.shard_map(
        body,
        mesh=mesh,
        in_specs=(P("head", "seq", None), P("head", "seq", None), P("head"), P("head"), P()),
        out_specs=P("head", "seq", None),
        check_vma=False,
    )
```

```python
import jax
import jax.numpy as jnp
from jax import lax
from jax.experimental import pallas as pl
from jax.experimental.pallas import tpu as pltpu
from jax.sharding import PartitionSpec as P

QH = 64
KV = 8
HD = 128
BLK = 128
NH = 8
NZ = 16
PLANE = 4
Q_DEV = 256
K_DEV = 384
PIECE = K_DEV // NH
KBD = K_DEV // BLK
PKB = PLANE * KBD
ROWS = 2 * PKB
HALF = NZ // 2
CHUNKS = 4
CHUNK = Q_DEV // CHUNKS
EARLY = 5
NEGATIVE = -1e30
SCALE2 = 1.4426950408889634 * HD**-0.5
MESH = pl.DeviceIdType.MESH


def kernel(
    q_ref, k_ref, pick_ref, off_ref, own_ref, o_ref,
    qall, kp, pick_out, picks, recv1, stage2, table, probs, tops, raw, maxes, prob_in, top_in, weighted,
    mass_out, mass_in, plane_out, plane_in,
    local_sem, greet, ring_send, ring_recv, leaf_send, leaf_recv, pk_send, pk_recv, s1_send, s1_recv, s2_send, s2_recv, s3_send, s3_recv,
    pr_send, pr_recv, tp_send, tp_recv, ms_send, ms_recv, pe_send, pe_recv,
):
    head = lax.axis_index("head")
    seq = lax.axis_index("seq")
    z = seq // PLANE
    cls = seq % PLANE
    xl = cls // 2
    core = cls % 2

    def wrap(other):
        return lax.rem(other + NZ, NZ)

    def at_z(other):
        return {"head": head, "seq": wrap(other) * PLANE + cls}

    def at_head(i):
        return {"head": lax.rem(head + i + NH, NH), "seq": seq}

    def at_pair(gi, xo):
        return {"head": lax.rem(head + gi + NH, NH), "seq": z * PLANE + lax.rem(xl + xo, 2) * 2 + core}

    def at_plane(c):
        return {"head": head, "seq": z * PLANE + lax.rem(c + PLANE, PLANE)}

    def remote(src, dst, send, recv, device):
        return pltpu.make_async_remote_copy(
            src_ref=src, dst_ref=dst, send_sem=send, recv_sem=recv,
            device_id=device, device_id_type=MESH,
        )

    def signal(sem, device):
        pl.semaphore_signal(sem, inc=1, device_id=device, device_id_type=MESH)

    barrier = pltpu.get_barrier_semaphore()
    s2_pairs = [(gi, xo) for gi in range(NH) for xo in range(2) if gi or xo]
    near = [at_z(z + 1), at_z(z - 1), at_z(z + 2), at_z(z - 2)]
    near += [at_pair(gi, xo) for gi, xo in s2_pairs]
    near += [{"head": head, "seq": z * PLANE + lax.rem(xl + xo, 2) * 2 + (1 - core)} for xo in range(2)]
    for device in near:
        signal(barrier, device)

    own_q = pltpu.make_async_copy(q_ref, qall.at[z], local_sem.at[0])
    own_k = pltpu.make_async_copy(k_ref.at[pl.ds(head * PIECE, PIECE), :], recv1.at[head], local_sem.at[1])
    own_q.start()
    own_k.start()
    picked = (pick_ref[0] // (QH // KV)).astype(jnp.float32)
    pick_out[...] = jnp.full((16, HD), picked, jnp.float32).astype(jnp.bfloat16)
    picks[head] = pick_out[...]

    pl.semaphore_wait(barrier, len(near))

    def sign_of(direction):
        return 1 - 2 * direction

    def chunk_rows(c):
        return pl.ds(c * CHUNK, CHUNK)

    def trunk_copy(direction, d, c):
        sign = sign_of(direction)
        ref = qall.at[wrap(z - sign * (d - 2)), chunk_rows(c), :]
        return remote(
            q_ref.at[chunk_rows(c), :] if d == 2 else ref, ref,
            ring_send.at[direction, d // 2 - 1, c], ring_recv.at[direction, d // 2 - 1, c], at_z(z + 2 * sign),
        )

    def trunk_arrival(direction, d, c):
        sign = sign_of(direction)
        ref = qall.at[wrap(z - sign * d), chunk_rows(c), :]
        return remote(
            ref, ref,
            ring_send.at[direction, d // 2 - 1, c], ring_recv.at[direction, d // 2 - 1, c], at_z(z - 2 * sign),
        )

    def leaf_copy(direction, d):
        sign = sign_of(direction)
        ref = qall.at[wrap(z - sign * (d - 1))]
        return remote(
            q_ref if d == 1 else ref, ref,
            leaf_send.at[direction, d // 2], leaf_recv.at[direction, d // 2], at_z(z + sign),
        )

    def leaf_arrival(direction, d):
        sign = sign_of(direction)
        ref = qall.at[wrap(z - sign * d)]
        return remote(
            ref, ref, leaf_send.at[direction, d // 2], leaf_recv.at[direction, d // 2], at_z(z - sign)
        )

    def serve(d, c):
        for direction in range(2):
            trunk_arrival(direction, d, c).wait_recv()
            if d + 2 < HALF:
                trunk_copy(direction, d + 2, c).start()
            elif isinstance(c, int):
                if c * 2 // CHUNKS == direction:
                    trunk_copy(direction, d + 2, c).start()
            else:
                @pl.when(c * 2 // CHUNKS == direction)
                def _():
                    trunk_copy(direction, d + 2, c).start()

    def serve_leaves(d):
        for direction in range(2):
            leaf_copy(direction, d).start()

    def trunk_step(d):
        for c in range(CHUNKS):
            serve(d, c)
        serve_leaves(d + 1)

    def wait_leaves(d):
        for direction in range(2):
            leaf_arrival(direction, d).wait_recv()

    def s1_copy(i):
        other = lax.rem(head + i, NH)
        return remote(
            k_ref.at[pl.ds(other * PIECE, PIECE), :], recv1.at[head], s1_send.at[i], s1_recv.at[i], at_head(i)
        )

    def s1_arrival(i):
        other = lax.rem(head - i + NH, NH)
        return remote(
            k_ref.at[pl.ds(other * PIECE, PIECE), :], recv1.at[other], s1_send.at[i], s1_recv.at[i], at_head(-i)
        )

    def pk_copy(i):
        return remote(pick_out, picks.at[head], pk_send.at[i], pk_recv.at[i], at_head(i))

    def pk_arrival(i):
        other = lax.rem(head - i + NH, NH)
        return remote(pick_out, picks.at[other], pk_send.at[i], pk_recv.at[i], at_head(-i))

    def s2_copy(gi, xo):
        other = lax.rem(head + gi, NH)
        return remote(
            stage2.at[other], kp.at[pl.ds(xl * K_DEV + head * PIECE, PIECE), :],
            s2_send.at[gi, xo], s2_recv.at[gi, xo], at_pair(gi, xo),
        )

    def s2_arrival(gi, xo):
        other = lax.rem(head - gi + NH, NH)
        start = lax.rem(xl + xo, 2) * K_DEV + other * PIECE
        return remote(
            stage2.at[other], kp.at[pl.ds(start, PIECE), :],
            s2_send.at[gi, xo], s2_recv.at[gi, xo], at_pair(-gi, xo),
        )

    def s3_copy():
        return remote(
            kp.at[pl.ds(0, 2 * K_DEV), :], kp.at[pl.ds(2 * K_DEV, 2 * K_DEV), :], s3_send.at[0], s3_recv.at[0],
            {"head": head, "seq": z * PLANE + xl * 2 + (1 - core)},
        )

    for direction in range(2):
        trunk_copy(direction, 2, 0).start()
    for i in range(1, NH):
        s1_copy(i).start()
        pk_copy(i).start()
    for c in range(1, CHUNKS):
        for direction in range(2):
            trunk_copy(direction, 2, c).start()
    serve_leaves(1)
    for side in range(2):
        signal(greet.at[0, side], at_z(z + 2 - 4 * side))

    key_local = lax.broadcasted_iota(jnp.int32, (BLK, BLK), 0)
    query_local = lax.broadcasted_iota(jnp.int32, (BLK, BLK), 1)
    table[0] = jnp.full((BLK, BLK), NEGATIVE, jnp.float32)
    table[1] = jnp.where(key_local <= query_local, 0.0, NEGATIVE)
    table[2] = jnp.zeros((BLK, BLK), jnp.float32)

    trunk_step(2)
    for side in range(2):
        pl.semaphore_wait(greet.at[0, side], 1)
    for side in range(2):
        signal(greet.at[1, side], at_z(z + 4 - 8 * side))
    own_k.wait()
    for i in range(1, NH):
        pk_arrival(i).wait_recv()
        s1_arrival(i).wait_recv()
    pieces = [recv1[m].astype(jnp.float32) for m in range(NH)]
    for g in range(NH):
        wanted = picks[g].astype(jnp.float32)[0:8]
        wanted = jnp.concatenate([wanted] * (PIECE // 8), axis=0)
        chosen = pieces[0]
        for m in range(1, NH):
            chosen = jnp.where(wanted == float(m), pieces[m], chosen)
        stage2[g] = chosen.astype(jnp.bfloat16)
    for gi, xo in s2_pairs:
        s2_copy(gi, xo).start()
    kp[pl.ds(xl * K_DEV + head * PIECE, PIECE), :] = stage2[head]
    trunk_step(4)
    for side in range(2):
        pl.semaphore_wait(greet.at[1, side], 1)
    wait_leaves(1)
    own_q.wait()
    for gi, xo in s2_pairs:
        s2_arrival(gi, xo).wait_recv()
    s3_copy().start()

    offset = off_ref[0]
    far = wrap(z + HALF)

    def pr_copy(r):
        return remote(probs.at[wrap(z + HALF + r)], prob_in.at[z], pr_send.at[r], pr_recv.at[r], at_z(z + r))

    def tp_copy(r):
        return remote(tops.at[wrap(z + HALF + r)], top_in.at[z], tp_send.at[r], tp_recv.at[r], at_z(z + r))

    def pr_arrival(r):
        source = wrap(z - r)
        return remote(probs.at[source], prob_in.at[source], pr_send.at[r], pr_recv.at[r], at_z(z - r))

    def tp_arrival(r):
        source = wrap(z - r)
        return remote(tops.at[source], top_in.at[source], tp_send.at[r], tp_recv.at[r], at_z(z - r))

    first = lax.broadcasted_iota(jnp.int32, (ROWS, BLK), 0) < PKB

    def signed_of(item):
        d = (item + 1) // 2
        return jnp.where(lax.rem(item, 2) == 1, -d, d)

    def scores(item, lo, hi):
        slot = wrap(z + signed_of(item))
        q = qall[slot]
        for kb in range(lo, hi):
            s = lax.dot_general(
                kp[kb * BLK:(kb + 1) * BLK, :], q, (((1,), (1,)), ((), ())),
                preferred_element_type=jnp.float32,
            )
            owner_core = core if kb < PKB // 2 else 1 - core
            place = z * PKB + (kb // KBD % 2 * 2 + owner_core) * KBD + kb % KBD
            for j in range(2):
                ahead = slot * 8 + cls * 2 + j + offset - place
                sj = s[:, j * BLK:(j + 1) * BLK] + table[jnp.clip(ahead + 1, 0, 2)]
                top = jnp.max(sj, axis=0, keepdims=True)
                row = j * PKB + kb
                maxes[item, row:row + 1, :] = top
                raw[item, row:row + 1, :] = jnp.sum(jnp.exp2((sj - top) * SCALE2), axis=0, keepdims=True)

    def close(item):
        slot = wrap(z + signed_of(item))
        every = maxes[item]
        top0 = jnp.max(jnp.where(first, every, NEGATIVE), axis=0, keepdims=True)
        top1 = jnp.max(jnp.where(first, NEGATIVE, every), axis=0, keepdims=True)
        tops[slot, 0:1, :] = top0
        tops[slot, 1:2, :] = top1
        probs[slot] = raw[item] * jnp.exp2((every - jnp.where(first, top0, top1)) * SCALE2)

    def send_sums(item):
        r = HALF + signed_of(item)
        pr_copy(r).start()
        tp_copy(r).start()

    def early(item, unused):
        scores(item, 0, PKB // 2)
        return unused

    def middle(item, unused):
        @pl.when(item >= 1)
        def _():
            serve(6, item - 1)

        close(jnp.maximum(item - 1, 0))
        scores(item, PKB // 2, PKB)

        @pl.when(item >= 1)
        def _():
            send_sums(item - 1)

        return unused

    def late(item, unused):
        @pl.when(item == EARLY)
        def _():
            serve_leaves(7)
            wait_leaves(3)

        @pl.when(item == 9)
        def _():
            wait_leaves(5)

        @pl.when(item == 13)
        def _():
            wait_leaves(7)

        @pl.when(item == 15)
        def _():
            for c in range(CHUNKS):
                trunk_arrival(c * 2 // CHUNKS, HALF, c).wait_recv()

        close(item - 1)
        scores(item, 0, PKB)
        send_sums(item - 1)
        return unused

    lax.fori_loop(0, EARLY, early, 0)
    s3_copy().wait_recv()
    lax.fori_loop(0, EARLY, middle, 0)
    lax.fori_loop(EARLY, 2 * HALF, late, 0)
    close(2 * HALF - 1)

    prob_in[z] = probs[far]
    top_in[z] = tops[far]
    for direction in range(2):
        for d in range(2, HALF, 2):
            for c in range(CHUNKS):
                trunk_copy(direction, d, c).wait_send()
        for d in range(1, HALF, 2):
            leaf_copy(direction, d).wait_send()
    for i in range(1, NH):
        pk_copy(i).wait_send()
        s1_copy(i).wait_send()
    for gi, xo in s2_pairs:
        s2_copy(gi, xo).wait_send()
    s3_copy().wait_send()
    for r in range(1, NZ):
        tp_arrival(r).wait_recv()
        pr_arrival(r).wait_recv()
    each = top_in[...]
    top = jnp.max(each, axis=0, keepdims=True)
    factor = jnp.exp2((each - top) * SCALE2)
    total = jnp.zeros((ROWS, BLK), jnp.float32)
    for source in range(NZ):
        part = prob_in[source] * jnp.where(first, factor[source, 0:1], factor[source, 1:2])
        total = total + part
        weighted[source * ROWS:(source + 1) * ROWS, :] = part
    sum0 = jnp.sum(jnp.where(first, total, 0.0), axis=0, keepdims=True)
    sum1 = jnp.sum(jnp.where(first, 0.0, total), axis=0, keepdims=True)
    inverse = 1.0 / jnp.where(lax.broadcasted_iota(jnp.int32, (8, BLK), 0) == 0, sum0, sum1)
    mass = lax.dot_general(
        inverse, weighted[...], (((1,), (1,)), ((), ())),
        precision=lax.Precision.HIGHEST, preferred_element_type=jnp.float32,
    )
    column = lax.broadcasted_iota(jnp.int32, (1, NZ * ROWS), 1)
    mass_out[...] = jnp.where(lax.rem(column, ROWS) < PKB, mass[0:1], mass[1:2])
    mass_in[far] = mass_out[...]

    def ms_copy(r):
        return remote(mass_out, mass_in.at[far], ms_send.at[r], ms_recv.at[r], at_z(z + r))

    def ms_arrival(r):
        source = wrap(z - r + HALF)
        return remote(mass_out, mass_in.at[source], ms_send.at[r], ms_recv.at[r], at_z(z - r))

    for d in range(HALF):
        ms_copy(HALF - d).start()
        if d:
            ms_copy(HALF + d).start()
    wide = lax.broadcasted_iota(jnp.int32, (8, NZ * ROWS), 1)
    sub = lax.broadcasted_iota(jnp.int32, (8, NZ * ROWS), 0)
    chosen = []
    for j in range(2):
        for c in range(0, PLANE, 2):
            place = jnp.full((8, NZ * ROWS), -1, jnp.int32)
            for row in range(8):
                if row % 4 < KBD:
                    block = own_ref[z * PKB + (c + row // 4) * KBD + row % 4]
                    device = lax.rem(block, PKB) // KBD
                    other_core = lax.rem(device + core, 2)
                    inner = (other_core * 2 + device // 2) * KBD + lax.rem(block, KBD)
                    lane = block // PKB * ROWS + j * PKB + inner
                    place = jnp.where(sub == row, lane, place)
            chosen.append(jnp.where(wide == place, 1.0, 0.0))
    chosen = jnp.concatenate(chosen, axis=0)
    for r in range(1, NZ):
        pr_copy(r).wait_send()
        tp_copy(r).wait_send()
    for c in range(CHUNKS):
        trunk_copy(c * 2 // CHUNKS, HALF, c).wait_send()
    for r in range(1, NZ):
        ms_arrival(r).wait_recv()
    spread = jnp.concatenate(
        [jnp.where(sub == 0, jnp.broadcast_to(mass_in[piece], (8, NZ * ROWS)), 0.0) for piece in range(NZ)], axis=0
    )
    rows = lax.dot_general(
        chosen, spread, (((1,), (1,)), ((), ())),
        precision=lax.Precision.HIGHEST, preferred_element_type=jnp.float32,
    )
    rows = pltpu.roll(rows[0:16] + pltpu.roll(rows[16:32], 1, 1), 2 * cls, 1)
    for c in range(PLANE):
        plane_out[c] = rows[4 * c:4 * c + 4]
    plane_in[cls] = plane_out[cls]

    def pe_copy(i):
        other = lax.rem(cls + i, PLANE)
        return remote(plane_out.at[other], plane_in.at[cls], pe_send.at[i], pe_recv.at[i], at_plane(cls + i))

    def pe_arrival(i):
        other = lax.rem(cls - i + PLANE, PLANE)
        return remote(plane_out.at[other], plane_in.at[other], pe_send.at[i], pe_recv.at[i], at_plane(cls - i))

    for i in range(1, PLANE):
        pe_copy(i).start()
    for r in range(1, NZ):
        ms_copy(r).wait_send()
    for i in range(1, PLANE):
        pe_arrival(i).wait_recv()
    final = plane_in[0] + plane_in[1] + plane_in[2] + plane_in[3]
    o_ref[0] = final[0:KBD]
    for i in range(1, PLANE):
        pe_copy(i).wait_send()


def body(queries, keys, head_pick, block_offset, owner_map):
    vmem = pl.BlockSpec(memory_space=pltpu.VMEM)
    smem = pl.BlockSpec(memory_space=pltpu.SMEM)
    hbm = pl.BlockSpec(memory_space=pl.ANY)
    f32, bf16 = jnp.float32, jnp.bfloat16
    dma = pltpu.SemaphoreType.DMA
    return pl.pallas_call(
        kernel,
        out_shape=jax.ShapeDtypeStruct((1, KBD, BLK), f32),
        in_specs=[hbm, hbm, smem, smem, smem],
        out_specs=vmem,
        scratch_shapes=[
            pltpu.VMEM((NZ, Q_DEV, HD), bf16),
            pltpu.VMEM((PLANE * K_DEV, HD), bf16),
            pltpu.VMEM((16, HD), bf16),
            pltpu.VMEM((NH, 16, HD), bf16),
            pltpu.VMEM((NH, PIECE, HD), bf16),
            pltpu.VMEM((NH, PIECE, HD), bf16),
            pltpu.VMEM((3, BLK, BLK), f32),
            pltpu.VMEM((NZ, ROWS, BLK), f32),
            pltpu.VMEM((NZ, 2, BLK), f32),
            pltpu.VMEM((NZ, ROWS, BLK), f32),
            pltpu.VMEM((NZ, ROWS, BLK), f32),
            pltpu.VMEM((NZ, ROWS, BLK), f32),
            pltpu.VMEM((NZ, 2, BLK), f32),
            pltpu.VMEM((NZ * ROWS, BLK), f32),
            pltpu.VMEM((1, NZ * ROWS), f32),
            pltpu.VMEM((NZ, 1, NZ * ROWS), f32),
            pltpu.VMEM((PLANE, 4, BLK), f32),
            pltpu.VMEM((PLANE, 4, BLK), f32),
            dma((2,)), pltpu.SemaphoreType.REGULAR((2, 2)),
            dma((2, HALF // 2, CHUNKS)), dma((2, HALF // 2, CHUNKS)),
            dma((2, HALF // 2)), dma((2, HALF // 2)),
            dma((NH,)), dma((NH,)),
            dma((NH,)), dma((NH,)),
            dma((NH, 2)), dma((NH, 2)),
            dma((1,)), dma((1,)),
            dma((NZ,)), dma((NZ,)),
            dma((NZ,)), dma((NZ,)),
            dma((NZ,)), dma((NZ,)),
            dma((PLANE,)), dma((PLANE,)),
        ],
        compiler_params=pltpu.CompilerParams(
            collective_id=0, has_side_effects=True, vmem_limit_bytes=60 * 1024 * 1024
        ),
        cost_estimate=pl.CostEstimate(flops=1610612736, bytes_accessed=165000, transcendentals=6291456),
    )(queries[0], keys[0], head_pick, block_offset, owner_map)


def solution(mesh):
    return jax.shard_map(
        body,
        mesh=mesh,
        in_specs=(P("head", "seq", None), P("head", "seq", None), P("head"), P("head"), P()),
        out_specs=P("head", "seq", None),
        check_vma=False,
    )
```

```python
import jax
import jax.numpy as jnp
from jax import lax
from jax.experimental import pallas as pl
from jax.experimental.pallas import tpu as pltpu
from jax.sharding import PartitionSpec as P

QH = 64
KV = 8
HD = 128
BLK = 128
NH = 8
NZ = 16
PLANE = 4
Q_DEV = 256
K_DEV = 384
PIECE = K_DEV // NH
KBD = K_DEV // BLK
PKB = PLANE * KBD
ROWS = 2 * PKB
HALF = NZ // 2
CHUNKS = 2
CHUNK = Q_DEV // CHUNKS
EARLY = 5
QBD = Q_DEV // BLK * PLANE
REACH = 64 + QBD - 1
NEGATIVE = -1e30
SCALE2 = 1.4426950408889634 * HD**-0.5
MESH = pl.DeviceIdType.MESH


def kernel(
    q_ref, k_ref, pick_hbm, off_hbm, own_hbm, o_ref,
    qall, kp, pick_out, picks, recv1, stage2, table, probs, tops, raw, maxes, prob_in, top_in, weighted,
    mass_out, mass_in, plane_out, plane_in,
    pick_ref, off_ref, own_ref, local_sem, greet, ring_send, ring_recv, leaf_send, leaf_recv, pk_send, pk_recv, s1_send, s1_recv, s2_send, s2_recv, s3_send, s3_recv,
    pr_send, pr_recv, tp_send, tp_recv, ms_send, ms_recv, pe_send, pe_recv,
):
    head = lax.axis_index("head")
    seq = lax.axis_index("seq")
    z = seq // PLANE
    cls = seq % PLANE
    xl = cls // 2
    core = cls % 2

    def wrap(other):
        return lax.rem(other + NZ, NZ)

    def at_z(other):
        return {"head": head, "seq": wrap(other) * PLANE + cls}

    def at_head(i):
        return {"head": lax.rem(head + i + NH, NH), "seq": seq}

    def at_pair(gi, xo):
        return {"head": lax.rem(head + gi + NH, NH), "seq": z * PLANE + lax.rem(xl + xo, 2) * 2 + core}

    def at_plane(c):
        return {"head": head, "seq": z * PLANE + lax.rem(c + PLANE, PLANE)}

    def remote(src, dst, send, recv, device):
        return pltpu.make_async_remote_copy(
            src_ref=src, dst_ref=dst, send_sem=send, recv_sem=recv,
            device_id=device, device_id_type=MESH,
        )

    def signal(sem, device):
        pl.semaphore_signal(sem, inc=1, device_id=device, device_id_type=MESH)

    barrier = pltpu.get_barrier_semaphore()
    s2_pairs = [(gi, xo) for gi in range(NH) for xo in range(2) if gi or xo]
    near = [at_z(z + 1), at_z(z - 1), at_z(z + 2), at_z(z - 2)]
    near += [at_pair(gi, xo) for gi, xo in s2_pairs]
    near += [{"head": head, "seq": z * PLANE + lax.rem(xl + xo, 2) * 2 + (1 - core)} for xo in range(2)]
    for device in near:
        signal(barrier, device)

    own_q = pltpu.make_async_copy(q_ref, qall.at[z], local_sem.at[0])
    own_k = pltpu.make_async_copy(k_ref.at[pl.ds(head * PIECE, PIECE), :], recv1.at[head], local_sem.at[1])
    scalars = [
        pltpu.make_async_copy(pick_hbm, pick_ref, local_sem.at[2]),
        pltpu.make_async_copy(off_hbm, off_ref, local_sem.at[3]),
        pltpu.make_async_copy(own_hbm, own_ref, local_sem.at[4]),
    ]
    for copy in scalars:
        copy.start()
    own_k.start()
    own_q.start()

    pl.semaphore_wait(barrier, len(near))

    def sign_of(direction):
        return 1 - 2 * direction

    def chunk_rows(c):
        return pl.ds(c * CHUNK, CHUNK)

    def trunk_copy(direction, d, c):
        sign = sign_of(direction)
        ref = qall.at[wrap(z - sign * (d - 2)), chunk_rows(c), :]
        return remote(
            q_ref.at[chunk_rows(c), :] if d == 2 else ref, ref,
            ring_send.at[direction, d // 2 - 1, c], ring_recv.at[direction, d // 2 - 1, c], at_z(z + 2 * sign),
        )

    def trunk_arrival(direction, d, c):
        sign = sign_of(direction)
        ref = qall.at[wrap(z - sign * d), chunk_rows(c), :]
        return remote(
            ref, ref,
            ring_send.at[direction, d // 2 - 1, c], ring_recv.at[direction, d // 2 - 1, c], at_z(z - 2 * sign),
        )

    def leaf_copy(direction, d):
        sign = sign_of(direction)
        ref = qall.at[wrap(z - sign * (d - 1))]
        return remote(
            q_ref if d == 1 else ref, ref,
            leaf_send.at[direction, d // 2], leaf_recv.at[direction, d // 2], at_z(z + sign),
        )

    def leaf_arrival(direction, d):
        sign = sign_of(direction)
        ref = qall.at[wrap(z - sign * d)]
        return remote(
            ref, ref, leaf_send.at[direction, d // 2], leaf_recv.at[direction, d // 2], at_z(z - sign)
        )

    def meets(query_plane, key_plane):
        return PKB * key_plane <= QBD * query_plane + REACH

    def comes(direction, d, query_plane):
        if direction == 1:
            return query_plane >= d
        if d % 2 == 0:
            return jnp.logical_or(query_plane >= HALF, meets(query_plane, query_plane + d))
        return jnp.logical_or(query_plane + d >= NZ, meets(query_plane, query_plane + d))

    def when(condition, action):
        @pl.when(condition)
        def _():
            action()

    def serve(d, c):
        for direction in range(2):
            piece = wrap(z - sign_of(direction) * d)
            goes_on = comes(direction, d + 2, piece)
            if d + 2 == HALF:
                goes_on = jnp.logical_and(goes_on, c * 2 // CHUNKS == direction)
            when(comes(direction, d, piece), trunk_arrival(direction, d, c).wait_recv)
            when(goes_on, trunk_copy(direction, d + 2, c).start)

    def serve_leaves(d):
        for direction in range(2):
            piece = wrap(z - sign_of(direction) * (d - 1))
            when(comes(direction, d, piece), leaf_copy(direction, d).start)

    def trunk_step(d):
        for c in range(CHUNKS):
            serve(d, c)
        serve_leaves(d + 1)

    def wait_leaves(d):
        for direction in range(2):
            piece = wrap(z - sign_of(direction) * d)
            when(comes(direction, d, piece), leaf_arrival(direction, d).wait_recv)

    def s1_copy(i):
        other = lax.rem(head + i, NH)
        return remote(
            k_ref.at[pl.ds(other * PIECE, PIECE), :], recv1.at[head], s1_send.at[i], s1_recv.at[i], at_head(i)
        )

    def s1_arrival(i):
        other = lax.rem(head - i + NH, NH)
        return remote(
            k_ref.at[pl.ds(other * PIECE, PIECE), :], recv1.at[other], s1_send.at[i], s1_recv.at[i], at_head(-i)
        )

    def pk_copy(i):
        return remote(pick_out, picks.at[head], pk_send.at[i], pk_recv.at[i], at_head(i))

    def pk_arrival(i):
        other = lax.rem(head - i + NH, NH)
        return remote(pick_out, picks.at[other], pk_send.at[i], pk_recv.at[i], at_head(-i))

    def s2_copy(gi, xo):
        other = lax.rem(head + gi, NH)
        return remote(
            stage2.at[other], kp.at[pl.ds(xl * K_DEV + head * PIECE, PIECE), :],
            s2_send.at[gi, xo], s2_recv.at[gi, xo], at_pair(gi, xo),
        )

    def s2_arrival(gi, xo):
        other = lax.rem(head - gi + NH, NH)
        start = lax.rem(xl + xo, 2) * K_DEV + other * PIECE
        return remote(
            stage2.at[other], kp.at[pl.ds(start, PIECE), :],
            s2_send.at[gi, xo], s2_recv.at[gi, xo], at_pair(-gi, xo),
        )

    def s3_copy():
        return remote(
            kp.at[pl.ds(0, 2 * K_DEV), :], kp.at[pl.ds(2 * K_DEV, 2 * K_DEV), :], s3_send.at[0], s3_recv.at[0],
            {"head": head, "seq": z * PLANE + xl * 2 + (1 - core)},
        )

    for direction in range(2):
        when(comes(direction, 2, z), trunk_copy(direction, 2, 0).start)
    for i in range(1, NH):
        s1_copy(i).start()
    for c in range(1, CHUNKS):
        for direction in range(2):
            when(comes(direction, 2, z), trunk_copy(direction, 2, c).start)
    serve_leaves(1)
    for copy in scalars:
        copy.wait()
    picked = (pick_ref[0] // (QH // KV)).astype(jnp.float32)
    pick_out[...] = jnp.full((16, HD), picked, jnp.float32).astype(jnp.bfloat16)
    picks[head] = pick_out[...]
    for i in range(1, NH):
        pk_copy(i).start()
    for side in range(2):
        signal(greet.at[0, side], at_z(z + 2 - 4 * side))

    key_local = lax.broadcasted_iota(jnp.int32, (BLK, BLK), 0)
    query_local = lax.broadcasted_iota(jnp.int32, (BLK, BLK), 1)
    table[0] = jnp.full((BLK, BLK), NEGATIVE, jnp.float32)
    table[1] = jnp.where(key_local <= query_local, 0.0, NEGATIVE)
    table[2] = jnp.zeros((BLK, BLK), jnp.float32)

    trunk_step(2)
    for side in range(2):
        pl.semaphore_wait(greet.at[0, side], 1)
    for side in range(2):
        signal(greet.at[1, side], at_z(z + 4 - 8 * side))
    own_k.wait()
    for i in range(1, NH):
        pk_arrival(i).wait_recv()
        s1_arrival(i).wait_recv()
    pieces = [recv1[m].astype(jnp.float32) for m in range(NH)]
    for g in range(NH):
        wanted = picks[g].astype(jnp.float32)[0:8]
        wanted = jnp.concatenate([wanted] * (PIECE // 8), axis=0)
        chosen = pieces[0]
        for m in range(1, NH):
            chosen = jnp.where(wanted == float(m), pieces[m], chosen)
        stage2[g] = chosen.astype(jnp.bfloat16)
    for gi, xo in s2_pairs:
        s2_copy(gi, xo).start()
    kp[pl.ds(xl * K_DEV + head * PIECE, PIECE), :] = stage2[head]
    trunk_step(4)
    for side in range(2):
        pl.semaphore_wait(greet.at[1, side], 1)
    wait_leaves(1)
    own_q.wait()
    for gi, xo in s2_pairs:
        s2_arrival(gi, xo).wait_recv()
    s3_copy().start()

    offset = off_ref[0]
    far = wrap(z + HALF)

    def pr_copy(r):
        return remote(probs.at[wrap(z + HALF + r)], prob_in.at[z], pr_send.at[r], pr_recv.at[r], at_z(z + r))

    def tp_copy(r):
        return remote(tops.at[wrap(z + HALF + r)], top_in.at[z], tp_send.at[r], tp_recv.at[r], at_z(z + r))

    def pr_arrival(r):
        source = wrap(z - r)
        return remote(probs.at[source], prob_in.at[source], pr_send.at[r], pr_recv.at[r], at_z(z - r))

    def tp_arrival(r):
        source = wrap(z - r)
        return remote(tops.at[source], top_in.at[source], tp_send.at[r], tp_recv.at[r], at_z(z - r))

    first = lax.broadcasted_iota(jnp.int32, (ROWS, BLK), 0) < PKB

    def signed_of(item):
        d = (item + 1) // 2
        return jnp.where(lax.rem(item, 2) == 1, -d, d)

    def scores(item, lo, hi):
        slot = wrap(z + signed_of(item))
        q = qall[slot]
        for kb in range(lo, hi):
            s = lax.dot_general(
                kp[kb * BLK:(kb + 1) * BLK, :], q, (((1,), (1,)), ((), ())),
                preferred_element_type=jnp.float32,
            )
            owner_core = core if kb < PKB // 2 else 1 - core
            place = z * PKB + (kb // KBD % 2 * 2 + owner_core) * KBD + kb % KBD
            for j in range(2):
                ahead = slot * 8 + cls * 2 + j + offset - place
                sj = s[:, j * BLK:(j + 1) * BLK] + table[jnp.clip(ahead + 1, 0, 2)]
                top = jnp.max(sj, axis=0, keepdims=True)
                row = j * PKB + kb
                maxes[item, row:row + 1, :] = top
                raw[item, row:row + 1, :] = jnp.sum(jnp.exp2((sj - top) * SCALE2), axis=0, keepdims=True)

    def close(item, slot):
        every = maxes[item]
        top0 = jnp.max(jnp.where(first, every, NEGATIVE), axis=0, keepdims=True)
        top1 = jnp.max(jnp.where(first, NEGATIVE, every), axis=0, keepdims=True)
        tops[slot, 0:1, :] = top0
        tops[slot, 1:2, :] = top1
        probs[slot] = raw[item] * jnp.exp2((every - jnp.where(first, top0, top1)) * SCALE2)

    def send_sums(item):
        r = HALF + signed_of(item)
        pr_copy(r).start()
        tp_copy(r).start()

    def wanted_item(item):
        return meets(wrap(z + signed_of(item)), z)

    def early(item, unused):
        when(wanted_item(item), lambda: scores(item, 0, PKB // 2))
        return unused

    def slot_of(item):
        return wrap(z + signed_of(item))

    def step(item, lo, closed=False):
        before = jnp.maximum(item - 1, 0)
        now, ended = wanted_item(item), wanted_item(before)
        ended = jnp.logical_and(ended, jnp.logical_not(closed))

        @pl.when(now)
        def _():
            close(before, jnp.where(closed, NZ, slot_of(before)))
            scores(item, lo, PKB)

        when(jnp.logical_and(jnp.logical_not(now), ended), lambda: close(before, slot_of(before)))
        when(jnp.logical_and(ended, item >= 1), lambda: send_sums(before))

    def middle(item, unused):
        when(jnp.logical_and(item >= 1, item < 1 + CHUNKS), lambda: serve(6, item - 1))
        step(item, PKB // 2)
        return unused

    def late(item, unused):
        @pl.when(item == EARLY)
        def _():
            serve_leaves(7)
            wait_leaves(3)

        waits = jnp.logical_or(item == 9, jnp.logical_or(item == 13, item == 15))

        @pl.when(jnp.logical_and(waits, wanted_item(item - 1)))
        def _():
            close(item - 1, slot_of(item - 1))
            send_sums(item - 1)

        @pl.when(item == 9)
        def _():
            wait_leaves(5)

        when(item == 13, lambda: wait_leaves(7))

        @pl.when(jnp.logical_and(item == 15, far >= HALF))
        def _():
            for c in range(CHUNKS):
                trunk_arrival(c * 2 // CHUNKS, HALF, c).wait_recv()

        step(item, 0, waits)
        return unused

    lax.fori_loop(0, EARLY, early, 0)
    s3_copy().wait_recv()
    lax.fori_loop(0, EARLY, middle, 0)
    lax.fori_loop(EARLY, 2 * HALF, late, 0)

    def no_sums(source):
        prob_in[source] = jnp.zeros((ROWS, BLK), jnp.float32)
        top_in[source] = jnp.full((2, BLK), NEGATIVE, jnp.float32)

    @pl.when(meets(far, z))
    def _():
        close(2 * HALF - 1, far)
        prob_in[z] = probs[far]
        top_in[z] = tops[far]

    when(jnp.logical_not(meets(far, z)), lambda: no_sums(z))
    for direction in range(2):
        for d in range(2, HALF, 2):
            for c in range(CHUNKS):
                piece = wrap(z - sign_of(direction) * (d - 2))
                when(comes(direction, d, piece), trunk_copy(direction, d, c).wait_send)
        for d in range(1, HALF, 2):
            piece = wrap(z - sign_of(direction) * (d - 1))
            when(comes(direction, d, piece), leaf_copy(direction, d).wait_send)
    for i in range(1, NH):
        pk_copy(i).wait_send()
        s1_copy(i).wait_send()
    for gi, xo in s2_pairs:
        s2_copy(gi, xo).wait_send()
    s3_copy().wait_send()
    for r in range(1, NZ):
        source = wrap(z - r)
        sent = meets(far, source)

        @pl.when(sent)
        def _():
            tp_arrival(r).wait_recv()
            pr_arrival(r).wait_recv()

        when(jnp.logical_not(sent), lambda: no_sums(source))
    each = top_in[...]
    top = jnp.max(each, axis=0, keepdims=True)
    factor = jnp.exp2((each - top) * SCALE2)
    total = jnp.zeros((ROWS, BLK), jnp.float32)
    for source in range(NZ):
        part = prob_in[source] * jnp.where(first, factor[source, 0:1], factor[source, 1:2])
        total = total + part
        weighted[source * ROWS:(source + 1) * ROWS, :] = part
    sum0 = jnp.sum(jnp.where(first, total, 0.0), axis=0, keepdims=True)
    sum1 = jnp.sum(jnp.where(first, 0.0, total), axis=0, keepdims=True)
    inverse = 1.0 / jnp.where(lax.broadcasted_iota(jnp.int32, (8, BLK), 0) == 0, sum0, sum1)
    mass = lax.dot_general(
        inverse, weighted[...], (((1,), (1,)), ((), ())),
        precision=lax.Precision.HIGHEST, preferred_element_type=jnp.float32,
    )
    column = lax.broadcasted_iota(jnp.int32, (1, NZ * ROWS), 1)
    mass_out[...] = jnp.where(lax.rem(column, ROWS) < PKB, mass[0:1], mass[1:2])
    mass_in[far] = mass_out[...]

    def ms_copy(r):
        return remote(mass_out, mass_in.at[far], ms_send.at[r], ms_recv.at[r], at_z(z + r))

    def ms_arrival(r):
        source = wrap(z - r + HALF)
        return remote(mass_out, mass_in.at[source], ms_send.at[r], ms_recv.at[r], at_z(z - r))

    for d in range(HALF):
        ms_copy(HALF - d).start()
        if d:
            ms_copy(HALF + d).start()
    wide = lax.broadcasted_iota(jnp.int32, (8, NZ * ROWS), 1)
    sub = lax.broadcasted_iota(jnp.int32, (8, NZ * ROWS), 0)
    chosen = []
    for j in range(2):
        for c in range(0, PLANE, 2):
            place = jnp.full((8, NZ * ROWS), -1, jnp.int32)
            for row in range(8):
                if row % 4 < KBD:
                    block = own_ref[z * PKB + (c + row // 4) * KBD + row % 4]
                    device = lax.rem(block, PKB) // KBD
                    other_core = lax.rem(device + core, 2)
                    inner = (other_core * 2 + device // 2) * KBD + lax.rem(block, KBD)
                    lane = block // PKB * ROWS + j * PKB + inner
                    place = jnp.where(sub == row, lane, place)
            chosen.append(jnp.where(wide == place, 1.0, 0.0))
    chosen = jnp.concatenate(chosen, axis=0)
    for r in range(1, NZ):
        @pl.when(meets(wrap(z + HALF + r), z))
        def _():
            pr_copy(r).wait_send()
            tp_copy(r).wait_send()

    for c in range(CHUNKS):
        direction = c * 2 // CHUNKS
        piece = wrap(z - sign_of(direction) * (HALF - 2))
        when(comes(direction, HALF, piece), trunk_copy(direction, HALF, c).wait_send)
    for r in range(1, NZ):
        ms_arrival(r).wait_recv()
    spread = jnp.concatenate(
        [jnp.where(sub == 0, jnp.broadcast_to(mass_in[piece], (8, NZ * ROWS)), 0.0) for piece in range(NZ)], axis=0
    )
    rows = lax.dot_general(
        chosen, spread, (((1,), (1,)), ((), ())),
        precision=lax.Precision.HIGHEST, preferred_element_type=jnp.float32,
    )
    rows = pltpu.roll(rows[0:16] + pltpu.roll(rows[16:32], 1, 1), 2 * cls, 1)
    for c in range(PLANE):
        plane_out[c] = rows[4 * c:4 * c + 4]
    plane_in[cls] = plane_out[cls]

    def pe_copy(i):
        other = lax.rem(cls + i, PLANE)
        return remote(plane_out.at[other], plane_in.at[cls], pe_send.at[i], pe_recv.at[i], at_plane(cls + i))

    def pe_arrival(i):
        other = lax.rem(cls - i + PLANE, PLANE)
        return remote(plane_out.at[other], plane_in.at[other], pe_send.at[i], pe_recv.at[i], at_plane(cls - i))

    for i in range(1, PLANE):
        pe_copy(i).start()
    for r in range(1, NZ):
        ms_copy(r).wait_send()
    for i in range(1, PLANE):
        pe_arrival(i).wait_recv()
    final = plane_in[0] + plane_in[1] + plane_in[2] + plane_in[3]
    o_ref[0] = final[0:KBD]
    for i in range(1, PLANE):
        pe_copy(i).wait_send()


def body(queries, keys, head_pick, block_offset, owner_map):
    vmem = pl.BlockSpec(memory_space=pltpu.VMEM)
    hbm = pl.BlockSpec(memory_space=pl.ANY)
    f32, bf16 = jnp.float32, jnp.bfloat16
    dma = pltpu.SemaphoreType.DMA
    return pl.pallas_call(
        kernel,
        out_shape=jax.ShapeDtypeStruct((1, KBD, BLK), f32),
        in_specs=[hbm] * 5,
        out_specs=vmem,
        scratch_shapes=[
            pltpu.VMEM((NZ, Q_DEV, HD), bf16),
            pltpu.VMEM((PLANE * K_DEV, HD), bf16),
            pltpu.VMEM((16, HD), bf16),
            pltpu.VMEM((NH, 16, HD), bf16),
            pltpu.VMEM((NH, PIECE, HD), bf16),
            pltpu.VMEM((NH, PIECE, HD), bf16),
            pltpu.VMEM((3, BLK, BLK), f32),
            pltpu.VMEM((NZ + 1, ROWS, BLK), f32),
            pltpu.VMEM((NZ + 1, 2, BLK), f32),
            pltpu.VMEM((NZ, ROWS, BLK), f32),
            pltpu.VMEM((NZ, ROWS, BLK), f32),
            pltpu.VMEM((NZ, ROWS, BLK), f32),
            pltpu.VMEM((NZ, 2, BLK), f32),
            pltpu.VMEM((NZ * ROWS, BLK), f32),
            pltpu.VMEM((1, NZ * ROWS), f32),
            pltpu.VMEM((NZ, 1, NZ * ROWS), f32),
            pltpu.VMEM((PLANE, 4, BLK), f32),
            pltpu.VMEM((PLANE, 4, BLK), f32),
            pltpu.SMEM((1,), jnp.int32),
            pltpu.SMEM((1,), jnp.int32),
            pltpu.SMEM((NZ * PKB,), jnp.int32),
            dma((5,)), pltpu.SemaphoreType.REGULAR((2, 2)),
            dma((2, HALF // 2, CHUNKS)), dma((2, HALF // 2, CHUNKS)),
            dma((2, HALF // 2)), dma((2, HALF // 2)),
            dma((NH,)), dma((NH,)),
            dma((NH,)), dma((NH,)),
            dma((NH, 2)), dma((NH, 2)),
            dma((1,)), dma((1,)),
            dma((NZ,)), dma((NZ,)),
            dma((NZ,)), dma((NZ,)),
            dma((NZ,)), dma((NZ,)),
            dma((PLANE,)), dma((PLANE,)),
        ],
        compiler_params=pltpu.CompilerParams(
            collective_id=0, has_side_effects=True, vmem_limit_bytes=60 * 1024 * 1024
        ),
        cost_estimate=pl.CostEstimate(flops=1610612736, bytes_accessed=165000, transcendentals=6291456),
    )(queries[0], keys[0], head_pick, block_offset, owner_map)


def solution(mesh):
    return jax.shard_map(
        body,
        mesh=mesh,
        in_specs=(P("head", "seq", None), P("head", "seq", None), P("head"), P("head"), P()),
        out_specs=P("head", "seq", None),
        check_vma=False,
    )
```

```python
import jax
import jax.numpy as jnp
from jax import lax
from jax.experimental import pallas as pl
from jax.experimental.pallas import tpu as pltpu
from jax.sharding import PartitionSpec as P

QH = 64
KV = 8
HD = 128
BLK = 128
NH = 8
NZ = 16
PLANE = 4
Q_DEV = 256
K_DEV = 384
PIECE = K_DEV // NH
KBD = K_DEV // BLK
PKB = PLANE * KBD
ROWS = 2 * PKB
HALF = NZ // 2
CHUNKS = 2
CHUNK = Q_DEV // CHUNKS
EARLY = 5
FORWARD = 6
QBD = Q_DEV // BLK * PLANE
REACH = 64 + QBD - 1
NEGATIVE = -1e30
SCALE2 = 1.4426950408889634 * HD**-0.5
MESH = pl.DeviceIdType.MESH


def kernel(
    q_ref, k_ref, pick_hbm, off_hbm, own_hbm, o_ref,
    qall, kp, pick_out, picks, recv1, stage2, table, probs, tops, raw, maxes, prob_in, top_in, weighted,
    mass_out, mass_in, plane_out, plane_in,
    pick_ref, off_ref, own_ref, local_sem, greet, ring_send, ring_recv, leaf_send, leaf_recv, pk_send, pk_recv, s1_send, s1_recv, s2_send, s2_recv, s3_send, s3_recv,
    pr_send, pr_recv, tp_send, tp_recv, ms_send, ms_recv, pe_send, pe_recv,
):
    head = lax.axis_index("head")
    seq = lax.axis_index("seq")
    z = seq // PLANE
    cls = seq % PLANE
    xl = cls // 2
    core = cls % 2

    def wrap(other):
        return lax.rem(other + NZ, NZ)

    def at_z(other):
        return {"head": head, "seq": wrap(other) * PLANE + cls}

    def at_head(i):
        return {"head": lax.rem(head + i + NH, NH), "seq": seq}

    def at_pair(gi, xo):
        return {"head": lax.rem(head + gi + NH, NH), "seq": z * PLANE + lax.rem(xl + xo, 2) * 2 + core}

    def at_plane(c):
        return {"head": head, "seq": z * PLANE + lax.rem(c + PLANE, PLANE)}

    def remote(src, dst, send, recv, device):
        return pltpu.make_async_remote_copy(
            src_ref=src, dst_ref=dst, send_sem=send, recv_sem=recv,
            device_id=device, device_id_type=MESH,
        )

    def signal(sem, device):
        pl.semaphore_signal(sem, inc=1, device_id=device, device_id_type=MESH)

    barrier = pltpu.get_barrier_semaphore()
    s2_pairs = [(gi, xo) for gi in range(NH) for xo in range(2) if gi or xo]
    near = [at_z(z + 1), at_z(z - 1), at_z(z + 2), at_z(z - 2)]
    near += [at_pair(gi, xo) for gi, xo in s2_pairs]
    near += [{"head": head, "seq": z * PLANE + lax.rem(xl + xo, 2) * 2 + (1 - core)} for xo in range(2)]
    for device in near:
        signal(barrier, device)

    own_q = pltpu.make_async_copy(q_ref, qall.at[z], local_sem.at[0])
    own_k = pltpu.make_async_copy(k_ref.at[pl.ds(head * PIECE, PIECE), :], recv1.at[head], local_sem.at[1])
    scalars = [
        pltpu.make_async_copy(pick_hbm, pick_ref, local_sem.at[2]),
        pltpu.make_async_copy(off_hbm, off_ref, local_sem.at[3]),
        pltpu.make_async_copy(own_hbm, own_ref, local_sem.at[4]),
    ]
    for copy in scalars:
        copy.start()
    own_k.start()
    own_q.start()

    pl.semaphore_wait(barrier, len(near))

    def sign_of(direction):
        return 1 - 2 * direction

    def chunk_rows(c):
        return pl.ds(c * CHUNK, CHUNK)

    def trunk_copy(direction, d, c):
        sign = sign_of(direction)
        ref = qall.at[wrap(z - sign * (d - 2)), chunk_rows(c), :]
        return remote(
            q_ref.at[chunk_rows(c), :] if d == 2 else ref, ref,
            ring_send.at[direction, d // 2 - 1, c], ring_recv.at[direction, d // 2 - 1, c], at_z(z + 2 * sign),
        )

    def trunk_arrival(direction, d, c):
        sign = sign_of(direction)
        ref = qall.at[wrap(z - sign * d), chunk_rows(c), :]
        return remote(
            ref, ref,
            ring_send.at[direction, d // 2 - 1, c], ring_recv.at[direction, d // 2 - 1, c], at_z(z - 2 * sign),
        )

    def leaf_copy(direction, d):
        sign = sign_of(direction)
        ref = qall.at[wrap(z - sign * (d - 1))]
        return remote(
            q_ref if d == 1 else ref, ref,
            leaf_send.at[direction, d // 2], leaf_recv.at[direction, d // 2], at_z(z + sign),
        )

    def leaf_arrival(direction, d):
        sign = sign_of(direction)
        ref = qall.at[wrap(z - sign * d)]
        return remote(
            ref, ref, leaf_send.at[direction, d // 2], leaf_recv.at[direction, d // 2], at_z(z - sign)
        )

    def meets(query_plane, key_plane):
        return PKB * key_plane <= QBD * query_plane + REACH

    def comes(direction, d, query_plane):
        if direction == 1:
            return query_plane >= d
        if d % 2 == 0:
            return jnp.logical_or(query_plane >= HALF, meets(query_plane, query_plane + d))
        return jnp.logical_or(query_plane + d >= NZ, meets(query_plane, query_plane + d))

    def when(condition, action):
        @pl.when(condition)
        def _():
            action()

    def serve(d, c):
        for direction in range(2):
            piece = wrap(z - sign_of(direction) * d)
            goes_on = comes(direction, d + 2, piece)
            if d + 2 == HALF:
                goes_on = jnp.logical_and(goes_on, c * 2 // CHUNKS == direction)
            when(comes(direction, d, piece), trunk_arrival(direction, d, c).wait_recv)
            when(goes_on, trunk_copy(direction, d + 2, c).start)

    def serve_leaves(d):
        for direction in range(2):
            piece = wrap(z - sign_of(direction) * (d - 1))
            when(comes(direction, d, piece), leaf_copy(direction, d).start)

    def trunk_step(d):
        for c in range(CHUNKS):
            serve(d, c)
        serve_leaves(d + 1)

    def wait_leaves(d):
        for direction in range(2):
            piece = wrap(z - sign_of(direction) * d)
            when(comes(direction, d, piece), leaf_arrival(direction, d).wait_recv)

    def s1_copy(i):
        other = lax.rem(head + i, NH)
        return remote(
            k_ref.at[pl.ds(other * PIECE, PIECE), :], recv1.at[head], s1_send.at[i], s1_recv.at[i], at_head(i)
        )

    def s1_arrival(i):
        other = lax.rem(head - i + NH, NH)
        return remote(
            k_ref.at[pl.ds(other * PIECE, PIECE), :], recv1.at[other], s1_send.at[i], s1_recv.at[i], at_head(-i)
        )

    def pk_copy(i):
        return remote(pick_out, picks.at[head], pk_send.at[i], pk_recv.at[i], at_head(i))

    def pk_arrival(i):
        other = lax.rem(head - i + NH, NH)
        return remote(pick_out, picks.at[other], pk_send.at[i], pk_recv.at[i], at_head(-i))

    def s2_copy(gi, xo):
        other = lax.rem(head + gi, NH)
        return remote(
            stage2.at[other], kp.at[pl.ds(xl * K_DEV + head * PIECE, PIECE), :],
            s2_send.at[gi, xo], s2_recv.at[gi, xo], at_pair(gi, xo),
        )

    def s2_arrival(gi, xo):
        other = lax.rem(head - gi + NH, NH)
        start = lax.rem(xl + xo, 2) * K_DEV + other * PIECE
        return remote(
            stage2.at[other], kp.at[pl.ds(start, PIECE), :],
            s2_send.at[gi, xo], s2_recv.at[gi, xo], at_pair(-gi, xo),
        )

    def s3_copy():
        return remote(
            kp.at[pl.ds(0, 2 * K_DEV), :], kp.at[pl.ds(2 * K_DEV, 2 * K_DEV), :], s3_send.at[0], s3_recv.at[0],
            {"head": head, "seq": z * PLANE + xl * 2 + (1 - core)},
        )

    for direction in range(2):
        when(comes(direction, 2, z), trunk_copy(direction, 2, 0).start)
    for i in range(1, NH):
        s1_copy(i).start()
    for c in range(1, CHUNKS):
        for direction in range(2):
            when(comes(direction, 2, z), trunk_copy(direction, 2, c).start)
    serve_leaves(1)
    for copy in scalars:
        copy.wait()
    picked = (pick_ref[0] // (QH // KV)).astype(jnp.float32)
    pick_out[...] = jnp.full((16, HD), picked, jnp.float32).astype(jnp.bfloat16)
    picks[head] = pick_out[...]
    for i in range(1, NH):
        pk_copy(i).start()
    for side in range(2):
        signal(greet.at[0, side], at_z(z + 2 - 4 * side))

    key_local = lax.broadcasted_iota(jnp.int32, (BLK, BLK), 0)
    query_local = lax.broadcasted_iota(jnp.int32, (BLK, BLK), 1)
    table[0] = jnp.full((BLK, BLK), NEGATIVE, jnp.float32)
    table[1] = jnp.where(key_local <= query_local, 0.0, NEGATIVE)
    table[2] = jnp.zeros((BLK, BLK), jnp.float32)

    trunk_step(2)
    for side in range(2):
        pl.semaphore_wait(greet.at[0, side], 1)
    for side in range(2):
        signal(greet.at[1, side], at_z(z + 4 - 8 * side))
    own_k.wait()
    for i in range(1, NH):
        pk_arrival(i).wait_recv()
        s1_arrival(i).wait_recv()
    pieces = [recv1[m].astype(jnp.float32) for m in range(NH)]
    for g in range(NH):
        wanted = picks[g].astype(jnp.float32)[0:8]
        wanted = jnp.concatenate([wanted] * (PIECE // 8), axis=0)
        chosen = pieces[0]
        for m in range(1, NH):
            chosen = jnp.where(wanted == float(m), pieces[m], chosen)
        stage2[g] = chosen.astype(jnp.bfloat16)
    for gi, xo in s2_pairs:
        s2_copy(gi, xo).start()
    kp[pl.ds(xl * K_DEV + head * PIECE, PIECE), :] = stage2[head]
    trunk_step(4)
    for side in range(2):
        pl.semaphore_wait(greet.at[1, side], 1)
    wait_leaves(1)
    own_q.wait()

    @pl.when(z >= FORWARD)
    def _():
        for c in range(CHUNKS):
            serve(6, c)
        serve_leaves(7)

    for gi, xo in s2_pairs:
        s2_arrival(gi, xo).wait_recv()
    s3_copy().start()

    offset = off_ref[0]
    far = wrap(z + HALF)

    def pr_copy(r):
        return remote(probs.at[wrap(z + HALF + r)], prob_in.at[z], pr_send.at[r], pr_recv.at[r], at_z(z + r))

    def tp_copy(r):
        return remote(tops.at[wrap(z + HALF + r)], top_in.at[z], tp_send.at[r], tp_recv.at[r], at_z(z + r))

    def pr_arrival(r):
        source = wrap(z - r)
        return remote(probs.at[source], prob_in.at[source], pr_send.at[r], pr_recv.at[r], at_z(z - r))

    def tp_arrival(r):
        source = wrap(z - r)
        return remote(tops.at[source], top_in.at[source], tp_send.at[r], tp_recv.at[r], at_z(z - r))

    first = lax.broadcasted_iota(jnp.int32, (ROWS, BLK), 0) < PKB

    def signed_of(item):
        d = (item + 1) // 2
        return jnp.where(lax.rem(item, 2) == 1, -d, d)

    def scores(item, lo, hi):
        slot = wrap(z + signed_of(item))
        q = qall[slot]
        for kb in range(lo, hi):
            s = lax.dot_general(
                kp[kb * BLK:(kb + 1) * BLK, :], q, (((1,), (1,)), ((), ())),
                preferred_element_type=jnp.float32,
            )
            owner_core = core if kb < PKB // 2 else 1 - core
            place = z * PKB + (kb // KBD % 2 * 2 + owner_core) * KBD + kb % KBD
            for j in range(2):
                ahead = slot * 8 + cls * 2 + j + offset - place
                sj = s[:, j * BLK:(j + 1) * BLK] + table[jnp.clip(ahead + 1, 0, 2)]
                top = jnp.max(sj, axis=0, keepdims=True)
                row = j * PKB + kb
                maxes[item, row:row + 1, :] = top
                raw[item, row:row + 1, :] = jnp.sum(jnp.exp2((sj - top) * SCALE2), axis=0, keepdims=True)

    def close(item, slot):
        every = maxes[item]
        top0 = jnp.max(jnp.where(first, every, NEGATIVE), axis=0, keepdims=True)
        top1 = jnp.max(jnp.where(first, NEGATIVE, every), axis=0, keepdims=True)
        tops[slot, 0:1, :] = top0
        tops[slot, 1:2, :] = top1
        probs[slot] = raw[item] * jnp.exp2((every - jnp.where(first, top0, top1)) * SCALE2)

    def send_sums(item):
        r = HALF + signed_of(item)
        pr_copy(r).start()
        tp_copy(r).start()

    def wanted_item(item):
        return meets(wrap(z + signed_of(item)), z)

    def early(item, unused):
        when(wanted_item(item), lambda: scores(item, 0, PKB // 2))
        return unused

    def slot_of(item):
        return wrap(z + signed_of(item))

    def step(item, lo, closed=False):
        before = jnp.maximum(item - 1, 0)
        now, ended = wanted_item(item), wanted_item(before)
        ended = jnp.logical_and(ended, jnp.logical_not(closed))

        @pl.when(now)
        def _():
            close(before, jnp.where(closed, NZ, slot_of(before)))
            scores(item, lo, PKB)

        when(jnp.logical_and(jnp.logical_not(now), ended), lambda: close(before, slot_of(before)))
        when(jnp.logical_and(ended, item >= 1), lambda: send_sums(before))

    def middle(item, unused):
        serving = jnp.logical_and(item >= 1, item < 1 + CHUNKS)
        when(jnp.logical_and(serving, z < FORWARD), lambda: serve(6, item - 1))
        step(item, PKB // 2)
        return unused

    def late(item, unused):
        @pl.when(item == EARLY)
        def _():
            when(z < FORWARD, lambda: serve_leaves(7))
            wait_leaves(3)

        waits = jnp.logical_or(item == 9, jnp.logical_or(item == 13, item == 15))

        @pl.when(jnp.logical_and(waits, wanted_item(item - 1)))
        def _():
            close(item - 1, slot_of(item - 1))
            send_sums(item - 1)

        @pl.when(item == 9)
        def _():
            wait_leaves(5)

        when(item == 13, lambda: wait_leaves(7))

        @pl.when(jnp.logical_and(item == 15, far >= HALF))
        def _():
            for c in range(CHUNKS):
                trunk_arrival(c * 2 // CHUNKS, HALF, c).wait_recv()

        step(item, 0, waits)
        return unused

    lax.fori_loop(0, EARLY, early, 0)
    s3_copy().wait_recv()
    lax.fori_loop(0, EARLY, middle, 0)
    lax.fori_loop(EARLY, 2 * HALF, late, 0)

    def no_sums(source):
        prob_in[source] = jnp.zeros((ROWS, BLK), jnp.float32)
        top_in[source] = jnp.full((2, BLK), NEGATIVE, jnp.float32)

    @pl.when(meets(far, z))
    def _():
        close(2 * HALF - 1, far)
        prob_in[z] = probs[far]
        top_in[z] = tops[far]

    when(jnp.logical_not(meets(far, z)), lambda: no_sums(z))
    for direction in range(2):
        for d in range(2, HALF, 2):
            for c in range(CHUNKS):
                piece = wrap(z - sign_of(direction) * (d - 2))
                when(comes(direction, d, piece), trunk_copy(direction, d, c).wait_send)
        for d in range(1, HALF, 2):
            piece = wrap(z - sign_of(direction) * (d - 1))
            when(comes(direction, d, piece), leaf_copy(direction, d).wait_send)
    for i in range(1, NH):
        pk_copy(i).wait_send()
        s1_copy(i).wait_send()
    for gi, xo in s2_pairs:
        s2_copy(gi, xo).wait_send()
    s3_copy().wait_send()
    for r in range(1, NZ):
        source = wrap(z - r)
        sent = meets(far, source)

        @pl.when(sent)
        def _():
            tp_arrival(r).wait_recv()
            pr_arrival(r).wait_recv()

        when(jnp.logical_not(sent), lambda: no_sums(source))
    each = top_in[...]
    top = jnp.max(each, axis=0, keepdims=True)
    factor = jnp.exp2((each - top) * SCALE2)
    total = jnp.zeros((ROWS, BLK), jnp.float32)
    for source in range(NZ):
        part = prob_in[source] * jnp.where(first, factor[source, 0:1], factor[source, 1:2])
        total = total + part
        weighted[source * ROWS:(source + 1) * ROWS, :] = part
    sum0 = jnp.sum(jnp.where(first, total, 0.0), axis=0, keepdims=True)
    sum1 = jnp.sum(jnp.where(first, 0.0, total), axis=0, keepdims=True)
    inverse = 1.0 / jnp.where(lax.broadcasted_iota(jnp.int32, (8, BLK), 0) == 0, sum0, sum1)
    mass = lax.dot_general(
        inverse, weighted[...], (((1,), (1,)), ((), ())),
        precision=lax.Precision.HIGHEST, preferred_element_type=jnp.float32,
    )
    column = lax.broadcasted_iota(jnp.int32, (1, NZ * ROWS), 1)
    mass_out[...] = jnp.where(lax.rem(column, ROWS) < PKB, mass[0:1], mass[1:2])
    mass_in[far] = mass_out[...]

    def ms_copy(r):
        return remote(mass_out, mass_in.at[far], ms_send.at[r], ms_recv.at[r], at_z(z + r))

    def ms_arrival(r):
        source = wrap(z - r + HALF)
        return remote(mass_out, mass_in.at[source], ms_send.at[r], ms_recv.at[r], at_z(z - r))

    for d in range(HALF):
        ms_copy(HALF - d).start()
        if d:
            ms_copy(HALF + d).start()
    wide = lax.broadcasted_iota(jnp.int32, (8, NZ * ROWS), 1)
    sub = lax.broadcasted_iota(jnp.int32, (8, NZ * ROWS), 0)
    chosen = []
    for j in range(2):
        for c in range(0, PLANE, 2):
            place = jnp.full((8, NZ * ROWS), -1, jnp.int32)
            for row in range(8):
                if row % 4 < KBD:
                    block = own_ref[z * PKB + (c + row // 4) * KBD + row % 4]
                    device = lax.rem(block, PKB) // KBD
                    other_core = lax.rem(device + core, 2)
                    inner = (other_core * 2 + device // 2) * KBD + lax.rem(block, KBD)
                    lane = block // PKB * ROWS + j * PKB + inner
                    place = jnp.where(sub == row, lane, place)
            chosen.append(jnp.where(wide == place, 1.0, 0.0))
    chosen = jnp.concatenate(chosen, axis=0)
    for r in range(1, NZ):
        @pl.when(meets(wrap(z + HALF + r), z))
        def _():
            pr_copy(r).wait_send()
            tp_copy(r).wait_send()

    for c in range(CHUNKS):
        direction = c * 2 // CHUNKS
        piece = wrap(z - sign_of(direction) * (HALF - 2))
        when(comes(direction, HALF, piece), trunk_copy(direction, HALF, c).wait_send)
    for r in range(1, NZ):
        ms_arrival(r).wait_recv()
    spread = jnp.concatenate(
        [jnp.where(sub == 0, jnp.broadcast_to(mass_in[piece], (8, NZ * ROWS)), 0.0) for piece in range(NZ)], axis=0
    )
    rows = lax.dot_general(
        chosen, spread, (((1,), (1,)), ((), ())),
        precision=lax.Precision.HIGHEST, preferred_element_type=jnp.float32,
    )
    rows = pltpu.roll(rows[0:16] + pltpu.roll(rows[16:32], 1, 1), 2 * cls, 1)
    for c in range(PLANE):
        plane_out[c] = rows[4 * c:4 * c + 4]
    plane_in[cls] = plane_out[cls]

    def pe_copy(i):
        other = lax.rem(cls + i, PLANE)
        return remote(plane_out.at[other], plane_in.at[cls], pe_send.at[i], pe_recv.at[i], at_plane(cls + i))

    def pe_arrival(i):
        other = lax.rem(cls - i + PLANE, PLANE)
        return remote(plane_out.at[other], plane_in.at[other], pe_send.at[i], pe_recv.at[i], at_plane(cls - i))

    for i in range(1, PLANE):
        pe_copy(i).start()
    for r in range(1, NZ):
        ms_copy(r).wait_send()
    for i in range(1, PLANE):
        pe_arrival(i).wait_recv()
    final = plane_in[0] + plane_in[1] + plane_in[2] + plane_in[3]
    o_ref[0] = final[0:KBD]
    for i in range(1, PLANE):
        pe_copy(i).wait_send()


def body(queries, keys, head_pick, block_offset, owner_map):
    vmem = pl.BlockSpec(memory_space=pltpu.VMEM)
    hbm = pl.BlockSpec(memory_space=pl.ANY)
    f32, bf16 = jnp.float32, jnp.bfloat16
    dma = pltpu.SemaphoreType.DMA
    return pl.pallas_call(
        kernel,
        out_shape=jax.ShapeDtypeStruct((1, KBD, BLK), f32),
        in_specs=[hbm] * 5,
        out_specs=vmem,
        scratch_shapes=[
            pltpu.VMEM((NZ, Q_DEV, HD), bf16),
            pltpu.VMEM((PLANE * K_DEV, HD), bf16),
            pltpu.VMEM((16, HD), bf16),
            pltpu.VMEM((NH, 16, HD), bf16),
            pltpu.VMEM((NH, PIECE, HD), bf16),
            pltpu.VMEM((NH, PIECE, HD), bf16),
            pltpu.VMEM((3, BLK, BLK), f32),
            pltpu.VMEM((NZ + 1, ROWS, BLK), f32),
            pltpu.VMEM((NZ + 1, 2, BLK), f32),
            pltpu.VMEM((NZ, ROWS, BLK), f32),
            pltpu.VMEM((NZ, ROWS, BLK), f32),
            pltpu.VMEM((NZ, ROWS, BLK), f32),
            pltpu.VMEM((NZ, 2, BLK), f32),
            pltpu.VMEM((NZ * ROWS, BLK), f32),
            pltpu.VMEM((1, NZ * ROWS), f32),
            pltpu.VMEM((NZ, 1, NZ * ROWS), f32),
            pltpu.VMEM((PLANE, 4, BLK), f32),
            pltpu.VMEM((PLANE, 4, BLK), f32),
            pltpu.SMEM((1,), jnp.int32),
            pltpu.SMEM((1,), jnp.int32),
            pltpu.SMEM((NZ * PKB,), jnp.int32),
            dma((5,)), pltpu.SemaphoreType.REGULAR((2, 2)),
            dma((2, HALF // 2, CHUNKS)), dma((2, HALF // 2, CHUNKS)),
            dma((2, HALF // 2)), dma((2, HALF // 2)),
            dma((NH,)), dma((NH,)),
            dma((NH,)), dma((NH,)),
            dma((NH, 2)), dma((NH, 2)),
            dma((1,)), dma((1,)),
            dma((NZ,)), dma((NZ,)),
            dma((NZ,)), dma((NZ,)),
            dma((NZ,)), dma((NZ,)),
            dma((PLANE,)), dma((PLANE,)),
        ],
        compiler_params=pltpu.CompilerParams(
            collective_id=0, has_side_effects=True, vmem_limit_bytes=60 * 1024 * 1024
        ),
        cost_estimate=pl.CostEstimate(flops=1610612736, bytes_accessed=165000, transcendentals=6291456),
    )(queries[0], keys[0], head_pick, block_offset, owner_map)


def solution(mesh):
    return jax.shard_map(
        body,
        mesh=mesh,
        in_specs=(P("head", "seq", None), P("head", "seq", None), P("head"), P("head"), P()),
        out_specs=P("head", "seq", None),
        check_vma=False,
    )
```

```python
import jax
import jax.numpy as jnp
from jax import lax
from jax.experimental import pallas as pl
from jax.experimental.pallas import tpu as pltpu
from jax.sharding import PartitionSpec as P

QH = 64
KV = 8
HD = 128
BLK = 128
NH = 8
NZ = 16
PLANE = 4
Q_DEV = 256
K_DEV = 384
PIECE = K_DEV // NH
KBD = K_DEV // BLK
PKB = PLANE * KBD
ROWS = 2 * PKB
HALF = NZ // 2
CHUNKS = 2
CHUNK = Q_DEV // CHUNKS
EARLY = 5
FORWARD = 6
QBD = Q_DEV // BLK * PLANE
REACH = 64 + QBD - 1
NEGATIVE = -1e30
SCALE2 = 1.4426950408889634 * HD**-0.5
MESH = pl.DeviceIdType.MESH


def kernel(
    q_ref, k_ref, pick_hbm, off_hbm, own_hbm, o_ref,
    qall, kp, pick_out, picks, recv1, stage2, table, probs, tops, raw, maxes, prob_in, top_in, weighted,
    mass_out, mass_in, plane_out, plane_in,
    pick_ref, off_ref, own_ref, local_sem, greet, ring_send, ring_recv, leaf_send, leaf_recv, pk_send, pk_recv, s1_send, s1_recv, s2_send, s2_recv, s3_send, s3_recv,
    pr_send, pr_recv, tp_send, tp_recv, ms_send, ms_recv, pe_send, pe_recv,
):
    head = lax.axis_index("head")
    seq = lax.axis_index("seq")
    z = seq // PLANE
    cls = seq % PLANE
    xl = cls // 2
    core = cls % 2

    def wrap(other):
        return lax.rem(other + NZ, NZ)

    def at_z(other):
        return {"head": head, "seq": wrap(other) * PLANE + cls}

    def at_head(i):
        return {"head": lax.rem(head + i + NH, NH), "seq": seq}

    def at_pair(gi, xo):
        return {"head": lax.rem(head + gi + NH, NH), "seq": z * PLANE + lax.rem(xl + xo, 2) * 2 + core}

    def remote(src, dst, send, recv, device):
        return pltpu.make_async_remote_copy(
            src_ref=src, dst_ref=dst, send_sem=send, recv_sem=recv,
            device_id=device, device_id_type=MESH,
        )

    def signal(sem, device):
        pl.semaphore_signal(sem, inc=1, device_id=device, device_id_type=MESH)

    barrier = pltpu.get_barrier_semaphore()
    s2_pairs = [(gi, xo) for gi in range(NH) for xo in range(2) if gi or xo]
    near = [at_z(z + 1), at_z(z - 1), at_z(z + 2), at_z(z - 2)]
    near += [at_pair(gi, xo) for gi, xo in s2_pairs]
    near += [{"head": head, "seq": z * PLANE + lax.rem(xl + xo, 2) * 2 + (1 - core)} for xo in range(2)]
    for device in near:
        signal(barrier, device)

    own_q = pltpu.make_async_copy(q_ref, qall.at[z], local_sem.at[0])
    own_k = pltpu.make_async_copy(k_ref.at[pl.ds(head * PIECE, PIECE), :], recv1.at[head], local_sem.at[1])
    scalars = [
        pltpu.make_async_copy(pick_hbm, pick_ref, local_sem.at[2]),
        pltpu.make_async_copy(off_hbm, off_ref, local_sem.at[3]),
        pltpu.make_async_copy(own_hbm, own_ref, local_sem.at[4]),
    ]
    for copy in scalars:
        copy.start()
    own_k.start()
    own_q.start()

    pl.semaphore_wait(barrier, len(near))

    def sign_of(direction):
        return 1 - 2 * direction

    def chunk_rows(c):
        return pl.ds(c * CHUNK, CHUNK)

    def trunk_copy(direction, d, c):
        sign = sign_of(direction)
        ref = qall.at[wrap(z - sign * (d - 2)), chunk_rows(c), :]
        return remote(
            q_ref.at[chunk_rows(c), :] if d == 2 else ref, ref,
            ring_send.at[direction, d // 2 - 1, c], ring_recv.at[direction, d // 2 - 1, c], at_z(z + 2 * sign),
        )

    def trunk_arrival(direction, d, c):
        sign = sign_of(direction)
        ref = qall.at[wrap(z - sign * d), chunk_rows(c), :]
        return remote(
            ref, ref,
            ring_send.at[direction, d // 2 - 1, c], ring_recv.at[direction, d // 2 - 1, c], at_z(z - 2 * sign),
        )

    def leaf_copy(direction, d):
        sign = sign_of(direction)
        ref = qall.at[wrap(z - sign * (d - 1))]
        return remote(
            q_ref if d == 1 else ref, ref,
            leaf_send.at[direction, d // 2], leaf_recv.at[direction, d // 2], at_z(z + sign),
        )

    def leaf_arrival(direction, d):
        sign = sign_of(direction)
        ref = qall.at[wrap(z - sign * d)]
        return remote(
            ref, ref, leaf_send.at[direction, d // 2], leaf_recv.at[direction, d // 2], at_z(z - sign)
        )

    def meets(query_plane, key_plane):
        return PKB * key_plane <= QBD * query_plane + REACH

    def comes(direction, d, query_plane):
        if direction == 1:
            return query_plane >= d
        if d % 2 == 0:
            return jnp.logical_or(query_plane >= HALF, meets(query_plane, query_plane + d))
        return jnp.logical_or(query_plane + d >= NZ, meets(query_plane, query_plane + d))

    def when(condition, action):
        @pl.when(condition)
        def _():
            action()

    def serve(d, c):
        for direction in range(2):
            piece = wrap(z - sign_of(direction) * d)
            goes_on = comes(direction, d + 2, piece)
            if d + 2 == HALF:
                goes_on = jnp.logical_and(goes_on, c * 2 // CHUNKS == direction)
            when(comes(direction, d, piece), trunk_arrival(direction, d, c).wait_recv)
            when(goes_on, trunk_copy(direction, d + 2, c).start)

    def serve_leaves(d):
        for direction in range(2):
            piece = wrap(z - sign_of(direction) * (d - 1))
            when(comes(direction, d, piece), leaf_copy(direction, d).start)

    def trunk_step(d):
        for c in range(CHUNKS):
            serve(d, c)
        serve_leaves(d + 1)

    def wait_leaves(d):
        for direction in range(2):
            piece = wrap(z - sign_of(direction) * d)
            when(comes(direction, d, piece), leaf_arrival(direction, d).wait_recv)

    def s1_copy(i):
        other = lax.rem(head + i, NH)
        return remote(
            k_ref.at[pl.ds(other * PIECE, PIECE), :], recv1.at[head], s1_send.at[i], s1_recv.at[i], at_head(i)
        )

    def s1_arrival(i):
        other = lax.rem(head - i + NH, NH)
        return remote(
            k_ref.at[pl.ds(other * PIECE, PIECE), :], recv1.at[other], s1_send.at[i], s1_recv.at[i], at_head(-i)
        )

    def pk_copy(i):
        return remote(pick_out, picks.at[head], pk_send.at[i], pk_recv.at[i], at_head(i))

    def pk_arrival(i):
        other = lax.rem(head - i + NH, NH)
        return remote(pick_out, picks.at[other], pk_send.at[i], pk_recv.at[i], at_head(-i))

    def s2_copy(gi, xo):
        other = lax.rem(head + gi, NH)
        return remote(
            stage2.at[other], kp.at[pl.ds(xl * K_DEV + head * PIECE, PIECE), :],
            s2_send.at[gi, xo], s2_recv.at[gi, xo], at_pair(gi, xo),
        )

    def s2_arrival(gi, xo):
        other = lax.rem(head - gi + NH, NH)
        start = lax.rem(xl + xo, 2) * K_DEV + other * PIECE
        return remote(
            stage2.at[other], kp.at[pl.ds(start, PIECE), :],
            s2_send.at[gi, xo], s2_recv.at[gi, xo], at_pair(-gi, xo),
        )

    def s3_copy():
        return remote(
            kp.at[pl.ds(0, 2 * K_DEV), :], kp.at[pl.ds(2 * K_DEV, 2 * K_DEV), :], s3_send.at[0], s3_recv.at[0],
            {"head": head, "seq": z * PLANE + xl * 2 + (1 - core)},
        )

    for c in range(CHUNKS):
        for direction in range(2):
            when(comes(direction, 2, z), trunk_copy(direction, 2, c).start)
    for i in range(1, NH):
        s1_copy(i).start()
    serve_leaves(1)
    for copy in scalars:
        copy.wait()
    picked = (pick_ref[0] // (QH // KV)).astype(jnp.float32)
    pick_out[...] = jnp.full((16, HD), picked, jnp.float32).astype(jnp.bfloat16)
    picks[head] = pick_out[...]
    for i in range(1, NH):
        pk_copy(i).start()
    for side in range(2):
        signal(greet.at[0, side], at_z(z + 2 - 4 * side))

    key_local = lax.broadcasted_iota(jnp.int32, (BLK, BLK), 0)
    query_local = lax.broadcasted_iota(jnp.int32, (BLK, BLK), 1)
    table[0] = jnp.full((BLK, BLK), NEGATIVE, jnp.float32)
    table[1] = jnp.where(key_local <= query_local, 0.0, NEGATIVE)
    table[2] = jnp.zeros((BLK, BLK), jnp.float32)

    trunk_step(2)
    for side in range(2):
        pl.semaphore_wait(greet.at[0, side], 1)
    for side in range(2):
        signal(greet.at[1, side], at_z(z + 4 - 8 * side))
    own_k.wait()
    for i in range(1, NH):
        pk_arrival(i).wait_recv()
        s1_arrival(i).wait_recv()
    pieces = [recv1[m].astype(jnp.float32) for m in range(NH)]
    for g in range(NH):
        wanted = picks[g].astype(jnp.float32)[0:8]
        wanted = jnp.concatenate([wanted] * (PIECE // 8), axis=0)
        chosen = pieces[0]
        for m in range(1, NH):
            chosen = jnp.where(wanted == float(m), pieces[m], chosen)
        stage2[g] = chosen.astype(jnp.bfloat16)
    for gi, xo in s2_pairs:
        s2_copy(gi, xo).start()
    kp[pl.ds(xl * K_DEV + head * PIECE, PIECE), :] = stage2[head]
    trunk_step(4)
    for side in range(2):
        pl.semaphore_wait(greet.at[1, side], 1)
    signal(greet.at[2, 0], at_pair(0, 1))
    wait_leaves(1)
    own_q.wait()

    @pl.when(z >= FORWARD)
    def _():
        for c in range(CHUNKS):
            serve(6, c)
        serve_leaves(7)

    for gi, xo in s2_pairs:
        s2_arrival(gi, xo).wait_recv()
    s3_copy().start()

    offset = off_ref[0]
    far = wrap(z + HALF)

    def pr_copy(r):
        return remote(probs.at[wrap(z + HALF + r)], prob_in.at[z], pr_send.at[r], pr_recv.at[r], at_z(z + r))

    def tp_copy(r):
        return remote(tops.at[wrap(z + HALF + r)], top_in.at[z], tp_send.at[r], tp_recv.at[r], at_z(z + r))

    def pr_arrival(r):
        source = wrap(z - r)
        return remote(probs.at[source], prob_in.at[source], pr_send.at[r], pr_recv.at[r], at_z(z - r))

    def tp_arrival(r):
        source = wrap(z - r)
        return remote(tops.at[source], top_in.at[source], tp_send.at[r], tp_recv.at[r], at_z(z - r))

    first = lax.broadcasted_iota(jnp.int32, (ROWS, BLK), 0) < PKB

    def signed_of(item):
        d = (item + 1) // 2
        return jnp.where(lax.rem(item, 2) == 1, -d, d)

    def scores(item, lo, hi, masked=True):
        slot = wrap(z + signed_of(item))
        q = qall[slot]
        for kb in range(lo, hi):
            s = lax.dot_general(
                kp[kb * BLK:(kb + 1) * BLK, :], q, (((1,), (1,)), ((), ())),
                preferred_element_type=jnp.float32,
            )
            owner_core = core if kb < PKB // 2 else 1 - core
            place = z * PKB + (kb // KBD % 2 * 2 + owner_core) * KBD + kb % KBD
            for j in range(2):
                ahead = slot * 8 + cls * 2 + j + offset - place
                sj = s[:, j * BLK:(j + 1) * BLK]
                if masked:
                    sj = sj + table[jnp.clip(ahead + 1, 0, 2)]
                top = jnp.max(sj, axis=0, keepdims=True)
                row = j * PKB + kb
                maxes[item, row:row + 1, :] = top
                raw[item, row:row + 1, :] = jnp.sum(jnp.exp2((sj - top) * SCALE2), axis=0, keepdims=True)

    def close(item, slot):
        every = maxes[item]
        top0 = jnp.max(jnp.where(first, every, NEGATIVE), axis=0, keepdims=True)
        top1 = jnp.max(jnp.where(first, NEGATIVE, every), axis=0, keepdims=True)
        tops[slot, 0:1, :] = top0
        tops[slot, 1:2, :] = top1
        probs[slot] = raw[item] * jnp.exp2((every - jnp.where(first, top0, top1)) * SCALE2)

    def send_sums(item):
        r = HALF + signed_of(item)
        pr_copy(r).start()
        tp_copy(r).start()

    def wanted_item(item):
        return meets(wrap(z + signed_of(item)), z)

    def early(item, unused):
        when(wanted_item(item), lambda: scores(item, 0, PKB // 2))
        return unused

    def slot_of(item):
        return wrap(z + signed_of(item))

    def step(item, lo, closed=False):
        before = jnp.maximum(item - 1, 0)
        now, ended = wanted_item(item), wanted_item(before)
        ended = jnp.logical_and(ended, jnp.logical_not(closed))

        whole = PKB * (z + 1) <= QBD * slot_of(item) + 2 * cls

        @pl.when(jnp.logical_and(now, whole))
        def _():
            close(before, jnp.where(closed, NZ, slot_of(before)))
            scores(item, lo, PKB, False)

        @pl.when(jnp.logical_and(now, jnp.logical_not(whole)))
        def _():
            close(before, jnp.where(closed, NZ, slot_of(before)))
            scores(item, lo, PKB)

        when(jnp.logical_and(jnp.logical_not(now), ended), lambda: close(before, slot_of(before)))
        when(jnp.logical_and(ended, item >= 1), lambda: send_sums(before))

    def middle(item, unused):
        serving = jnp.logical_and(item >= 1, item < 1 + CHUNKS)
        when(jnp.logical_and(serving, z < FORWARD), lambda: serve(6, item - 1))
        step(item, PKB // 2)
        return unused

    def late(item, unused):
        @pl.when(item == EARLY)
        def _():
            when(z < FORWARD, lambda: serve_leaves(7))
            wait_leaves(3)

        waits = jnp.logical_or(item == 9, jnp.logical_or(item == 13, item == 15))

        @pl.when(jnp.logical_and(waits, wanted_item(item - 1)))
        def _():
            close(item - 1, slot_of(item - 1))
            send_sums(item - 1)

        @pl.when(item == 9)
        def _():
            wait_leaves(5)

        when(item == 13, lambda: wait_leaves(7))

        @pl.when(jnp.logical_and(item == 15, far >= HALF))
        def _():
            for c in range(CHUNKS):
                trunk_arrival(c * 2 // CHUNKS, HALF, c).wait_recv()

        step(item, 0, waits)
        return unused

    lax.fori_loop(0, EARLY, early, 0)
    s3_copy().wait_recv()
    lax.fori_loop(0, EARLY, middle, 0)
    lax.fori_loop(EARLY, 2 * HALF, late, 0)

    def no_sums(source):
        prob_in[source] = jnp.zeros((ROWS, BLK), jnp.float32)
        top_in[source] = jnp.full((2, BLK), NEGATIVE, jnp.float32)

    @pl.when(meets(far, z))
    def _():
        close(2 * HALF - 1, far)
        prob_in[z] = probs[far]
        top_in[z] = tops[far]

    when(jnp.logical_not(meets(far, z)), lambda: no_sums(z))
    for direction in range(2):
        for d in range(2, HALF, 2):
            for c in range(CHUNKS):
                piece = wrap(z - sign_of(direction) * (d - 2))
                when(comes(direction, d, piece), trunk_copy(direction, d, c).wait_send)
        for d in range(1, HALF, 2):
            piece = wrap(z - sign_of(direction) * (d - 1))
            when(comes(direction, d, piece), leaf_copy(direction, d).wait_send)
    for i in range(1, NH):
        pk_copy(i).wait_send()
        s1_copy(i).wait_send()
    for gi, xo in s2_pairs:
        s2_copy(gi, xo).wait_send()
    s3_copy().wait_send()
    for r in range(1, NZ):
        source = wrap(z - r)
        sent = meets(far, source)

        @pl.when(sent)
        def _():
            tp_arrival(r).wait_recv()
            pr_arrival(r).wait_recv()

        when(jnp.logical_not(sent), lambda: no_sums(source))
    each = top_in[...]
    top = jnp.max(each, axis=0, keepdims=True)
    factor = jnp.exp2((each - top) * SCALE2)
    total = jnp.zeros((ROWS, BLK), jnp.float32)
    for source in range(NZ):
        part = prob_in[source] * jnp.where(first, factor[source, 0:1], factor[source, 1:2])
        total = total + part
        weighted[source * ROWS:(source + 1) * ROWS, :] = part
    sum0 = jnp.sum(jnp.where(first, total, 0.0), axis=0, keepdims=True)
    sum1 = jnp.sum(jnp.where(first, 0.0, total), axis=0, keepdims=True)
    inverse = 1.0 / jnp.where(lax.broadcasted_iota(jnp.int32, (8, BLK), 0) == 0, sum0, sum1)
    mass = lax.dot_general(
        inverse, weighted[...], (((1,), (1,)), ((), ())),
        precision=lax.Precision.HIGHEST, preferred_element_type=jnp.float32,
    )
    column = lax.broadcasted_iota(jnp.int32, (1, NZ * ROWS), 1)
    mass_out[...] = jnp.where(lax.rem(column, ROWS) < PKB, mass[0:1], mass[1:2])
    mass_in[xl, far] = mass_out[...]

    def at_line(xo, r):
        return {"head": head, "seq": wrap(z + r) * PLANE + lax.rem(xl + xo, 2) * 2 + core}

    def ms_copy(xo, r):
        return remote(mass_out, mass_in.at[xl, far], ms_send.at[xo, r], ms_recv.at[xo, r], at_line(xo, r))

    def ms_arrival(xo, r):
        slot = mass_in.at[lax.rem(xl + xo, 2), wrap(z - r + HALF)]
        return remote(mass_out, slot, ms_send.at[xo, r], ms_recv.at[xo, r], at_line(xo, -r))

    crossings = [(xo, r) for d in range(HALF) for r in ((HALF - d, HALF + d) if d else (HALF,)) for xo in range(2)]
    crossings.append((1, 0))
    pl.semaphore_wait(greet.at[2, 0], 1)
    for xo, r in crossings:
        ms_copy(xo, r).start()
    wide = lax.broadcasted_iota(jnp.int32, (8, NZ * ROWS), 1)
    sub = lax.broadcasted_iota(jnp.int32, (8, NZ * ROWS), 0)
    chosen = []
    for j in range(2):
        place = jnp.full((8, NZ * ROWS), -1, jnp.int32)
        for row in range(8):
            if row % 4 < KBD:
                block = own_ref[z * PKB + (xl * 2 + row // 4) * KBD + row % 4]
                device = lax.rem(block, PKB) // KBD
                other_core = lax.rem(device + core, 2)
                inner = (other_core * 2 + device // 2) * KBD + lax.rem(block, KBD)
                lane = block // PKB * ROWS + j * PKB + inner
                place = jnp.where(sub == row, lane, place)
        chosen.append(jnp.where(wide == place, 1.0, 0.0))
    chosen = jnp.concatenate(chosen, axis=0)
    for r in range(1, NZ):
        @pl.when(meets(wrap(z + HALF + r), z))
        def _():
            pr_copy(r).wait_send()
            tp_copy(r).wait_send()

    for c in range(CHUNKS):
        direction = c * 2 // CHUNKS
        piece = wrap(z - sign_of(direction) * (HALF - 2))
        when(comes(direction, HALF, piece), trunk_copy(direction, HALF, c).wait_send)
    for xo, r in crossings:
        ms_arrival(xo, r).wait_recv()
    spread = jnp.concatenate(
        [
            jnp.where(sub == 0, jnp.broadcast_to(mass_in[x, piece], (8, NZ * ROWS)), 0.0)
            for x in range(2) for piece in range(NZ)
        ],
        axis=0,
    )
    rows = lax.dot_general(
        chosen, spread, (((1,), (1,)), ((), ())),
        precision=lax.Precision.HIGHEST, preferred_element_type=jnp.float32,
    )
    rows = rows[0:8] + pltpu.roll(rows[8:16], 1, 1)
    rows = pltpu.roll(rows[:, 0:BLK], 2 * core, 1) + pltpu.roll(rows[:, BLK:2 * BLK], 4 + 2 * core, 1)
    for c in range(2):
        plane_out[c] = rows[4 * c:4 * c + 4]
    plane_in[core] = plane_out[core]

    def pe_copy():
        return remote(
            plane_out.at[1 - core], plane_in.at[core], pe_send.at[0], pe_recv.at[0],
            {"head": head, "seq": z * PLANE + xl * 2 + (1 - core)},
        )

    def pe_arrival():
        return remote(
            plane_out.at[1 - core], plane_in.at[1 - core], pe_send.at[0], pe_recv.at[0],
            {"head": head, "seq": z * PLANE + xl * 2 + (1 - core)},
        )

    pe_copy().start()
    for xo, r in crossings:
        ms_copy(xo, r).wait_send()
    pe_arrival().wait_recv()
    final = plane_in[0] + plane_in[1]
    o_ref[0] = final[0:KBD]
    pe_copy().wait_send()


def body(queries, keys, head_pick, block_offset, owner_map):
    vmem = pl.BlockSpec(memory_space=pltpu.VMEM)
    hbm = pl.BlockSpec(memory_space=pl.ANY)
    f32, bf16 = jnp.float32, jnp.bfloat16
    dma = pltpu.SemaphoreType.DMA
    return pl.pallas_call(
        kernel,
        out_shape=jax.ShapeDtypeStruct((1, KBD, BLK), f32),
        in_specs=[hbm] * 5,
        out_specs=vmem,
        scratch_shapes=[
            pltpu.VMEM((NZ, Q_DEV, HD), bf16),
            pltpu.VMEM((PLANE * K_DEV, HD), bf16),
            pltpu.VMEM((16, HD), bf16),
            pltpu.VMEM((NH, 16, HD), bf16),
            pltpu.VMEM((NH, PIECE, HD), bf16),
            pltpu.VMEM((NH, PIECE, HD), bf16),
            pltpu.VMEM((3, BLK, BLK), f32),
            pltpu.VMEM((NZ + 1, ROWS, BLK), f32),
            pltpu.VMEM((NZ + 1, 2, BLK), f32),
            pltpu.VMEM((NZ, ROWS, BLK), f32),
            pltpu.VMEM((NZ, ROWS, BLK), f32),
            pltpu.VMEM((NZ, ROWS, BLK), f32),
            pltpu.VMEM((NZ, 2, BLK), f32),
            pltpu.VMEM((NZ * ROWS, BLK), f32),
            pltpu.VMEM((1, NZ * ROWS), f32),
            pltpu.VMEM((2, NZ, 1, NZ * ROWS), f32),
            pltpu.VMEM((2, 4, BLK), f32),
            pltpu.VMEM((2, 4, BLK), f32),
            pltpu.SMEM((1,), jnp.int32),
            pltpu.SMEM((1,), jnp.int32),
            pltpu.SMEM((NZ * PKB,), jnp.int32),
            dma((5,)), pltpu.SemaphoreType.REGULAR((3, 2)),
            dma((2, HALF // 2, CHUNKS)), dma((2, HALF // 2, CHUNKS)),
            dma((2, HALF // 2)), dma((2, HALF // 2)),
            dma((NH,)), dma((NH,)),
            dma((NH,)), dma((NH,)),
            dma((NH, 2)), dma((NH, 2)),
            dma((1,)), dma((1,)),
            dma((NZ,)), dma((NZ,)),
            dma((NZ,)), dma((NZ,)),
            dma((2, NZ)), dma((2, NZ)),
            dma((1,)), dma((1,)),
        ],
        compiler_params=pltpu.CompilerParams(
            collective_id=0, has_side_effects=True, vmem_limit_bytes=60 * 1024 * 1024
        ),
        cost_estimate=pl.CostEstimate(flops=1610612736, bytes_accessed=165000, transcendentals=6291456),
    )(queries[0], keys[0], head_pick, block_offset, owner_map)


def solution(mesh):
    return jax.shard_map(
        body,
        mesh=mesh,
        in_specs=(P("head", "seq", None), P("head", "seq", None), P("head"), P("head"), P()),
        out_specs=P("head", "seq", None),
        check_vma=False,
    )
```

```python
import jax
import jax.numpy as jnp
from jax import lax
from jax.experimental import pallas as pl
from jax.experimental.pallas import tpu as pltpu
from jax.sharding import PartitionSpec as P

QH = 64
KV = 8
HD = 128
BLK = 128
NH = 8
NZ = 16
PLANE = 4
Q_DEV = 256
K_DEV = 384
PIECE = K_DEV // NH
KBD = K_DEV // BLK
PKB = PLANE * KBD
ROWS = 2 * PKB
HALF = NZ // 2
CHUNKS = 2
CHUNK = Q_DEV // CHUNKS
EARLY = 5
FORWARD = 6
QBD = Q_DEV // BLK * PLANE
REACH = 64 + QBD - 1
NEGATIVE = -1e30
SCALE2 = 1.4426950408889634 * HD**-0.5
MESH = pl.DeviceIdType.MESH


def kernel(
    q_ref, k_ref, pick_hbm, off_hbm, own_hbm, o_ref,
    qall, kp, pick_out, picks, recv1, stage2, table, probs, tops, raw, maxes, prob_in, top_in, weighted,
    mass_out, mass_in, plane_out, plane_in,
    pick_ref, off_ref, own_ref, local_sem, greet, ring_send, ring_recv, leaf_send, leaf_recv, pk_send, pk_recv, s1_send, s1_recv, s2_send, s2_recv, s3_send, s3_recv,
    pr_send, pr_recv, tp_send, tp_recv, ms_send, ms_recv, pe_send, pe_recv,
):
    head = lax.axis_index("head")
    seq = lax.axis_index("seq")
    z = seq // PLANE
    cls = seq % PLANE
    xl = cls // 2
    core = cls % 2

    def wrap(other):
        return lax.rem(other + NZ, NZ)

    def at_z(other):
        return {"head": head, "seq": wrap(other) * PLANE + cls}

    def at_head(i):
        return {"head": lax.rem(head + i + NH, NH), "seq": seq}

    def at_pair(gi, xo):
        return {"head": lax.rem(head + gi + NH, NH), "seq": z * PLANE + lax.rem(xl + xo, 2) * 2 + core}

    def remote(src, dst, send, recv, device):
        return pltpu.make_async_remote_copy(
            src_ref=src, dst_ref=dst, send_sem=send, recv_sem=recv,
            device_id=device, device_id_type=MESH,
        )

    def signal(sem, device):
        pl.semaphore_signal(sem, inc=1, device_id=device, device_id_type=MESH)

    barrier = pltpu.get_barrier_semaphore()
    s2_pairs = [(gi, xo) for gi in range(NH) for xo in range(2) if gi or xo]
    near = [at_z(z + 1), at_z(z - 1), at_z(z + 2), at_z(z - 2)]
    near += [at_pair(gi, xo) for gi, xo in s2_pairs]
    near += [{"head": head, "seq": z * PLANE + lax.rem(xl + xo, 2) * 2 + (1 - core)} for xo in range(2)]
    for device in near:
        signal(barrier, device)

    own_q = pltpu.make_async_copy(q_ref, qall.at[z], local_sem.at[0])
    own_k = pltpu.make_async_copy(k_ref.at[pl.ds(head * PIECE, PIECE), :], recv1.at[head], local_sem.at[1])
    scalars = [
        pltpu.make_async_copy(pick_hbm, pick_ref, local_sem.at[2]),
        pltpu.make_async_copy(off_hbm, off_ref, local_sem.at[3]),
        pltpu.make_async_copy(own_hbm, own_ref, local_sem.at[4]),
    ]
    for copy in scalars:
        copy.start()
    own_k.start()
    own_q.start()

    pl.semaphore_wait(barrier, len(near))

    def sign_of(direction):
        return 1 - 2 * direction

    def chunk_rows(c):
        return pl.ds(c * CHUNK, CHUNK)

    def trunk_copy(direction, d, c):
        sign = sign_of(direction)
        ref = qall.at[wrap(z - sign * (d - 2)), chunk_rows(c), :]
        return remote(
            q_ref.at[chunk_rows(c), :] if d == 2 else ref, ref,
            ring_send.at[direction, d // 2 - 1, c], ring_recv.at[direction, d // 2 - 1, c], at_z(z + 2 * sign),
        )

    def trunk_arrival(direction, d, c):
        sign = sign_of(direction)
        ref = qall.at[wrap(z - sign * d), chunk_rows(c), :]
        return remote(
            ref, ref,
            ring_send.at[direction, d // 2 - 1, c], ring_recv.at[direction, d // 2 - 1, c], at_z(z - 2 * sign),
        )

    def leaf_copy(direction, d):
        sign = sign_of(direction)
        ref = qall.at[wrap(z - sign * (d - 1))]
        return remote(
            q_ref if d == 1 else ref, ref,
            leaf_send.at[direction, d // 2], leaf_recv.at[direction, d // 2], at_z(z + sign),
        )

    def leaf_arrival(direction, d):
        sign = sign_of(direction)
        ref = qall.at[wrap(z - sign * d)]
        return remote(
            ref, ref, leaf_send.at[direction, d // 2], leaf_recv.at[direction, d // 2], at_z(z - sign)
        )

    def meets(query_plane, key_plane):
        return PKB * key_plane <= QBD * query_plane + REACH

    def comes(direction, d, query_plane):
        if direction == 1:
            return query_plane >= d
        if d % 2 == 0:
            return jnp.logical_or(query_plane >= HALF, meets(query_plane, query_plane + d))
        return jnp.logical_or(query_plane + d >= NZ, meets(query_plane, query_plane + d))

    def when(condition, action):
        @pl.when(condition)
        def _():
            action()

    def serve(d, c):
        for direction in range(2):
            piece = wrap(z - sign_of(direction) * d)
            goes_on = comes(direction, d + 2, piece)
            if d + 2 == HALF:
                goes_on = jnp.logical_and(goes_on, c * 2 // CHUNKS == direction)
            when(comes(direction, d, piece), trunk_arrival(direction, d, c).wait_recv)
            when(goes_on, trunk_copy(direction, d + 2, c).start)

    def serve_leaves(d):
        for direction in range(2):
            piece = wrap(z - sign_of(direction) * (d - 1))
            when(comes(direction, d, piece), leaf_copy(direction, d).start)

    def trunk_step(d):
        for c in range(CHUNKS):
            serve(d, c)
        serve_leaves(d + 1)

    def wait_leaves(d):
        for direction in range(2):
            piece = wrap(z - sign_of(direction) * d)
            when(comes(direction, d, piece), leaf_arrival(direction, d).wait_recv)

    def s1_copy(i):
        other = lax.rem(head + i, NH)
        return remote(
            k_ref.at[pl.ds(other * PIECE, PIECE), :], recv1.at[head], s1_send.at[i], s1_recv.at[i], at_head(i)
        )

    def s1_arrival(i):
        other = lax.rem(head - i + NH, NH)
        return remote(
            k_ref.at[pl.ds(other * PIECE, PIECE), :], recv1.at[other], s1_send.at[i], s1_recv.at[i], at_head(-i)
        )

    def pk_copy(i):
        return remote(pick_out, picks.at[head], pk_send.at[i], pk_recv.at[i], at_head(i))

    def pk_arrival(i):
        other = lax.rem(head - i + NH, NH)
        return remote(pick_out, picks.at[other], pk_send.at[i], pk_recv.at[i], at_head(-i))

    def s2_copy(gi, xo):
        other = lax.rem(head + gi, NH)
        return remote(
            stage2.at[other], kp.at[pl.ds(xl * K_DEV + head * PIECE, PIECE), :],
            s2_send.at[gi, xo], s2_recv.at[gi, xo], at_pair(gi, xo),
        )

    def s2_arrival(gi, xo):
        other = lax.rem(head - gi + NH, NH)
        start = lax.rem(xl + xo, 2) * K_DEV + other * PIECE
        return remote(
            stage2.at[other], kp.at[pl.ds(start, PIECE), :],
            s2_send.at[gi, xo], s2_recv.at[gi, xo], at_pair(-gi, xo),
        )

    def s3_copy():
        return remote(
            kp.at[pl.ds(0, 2 * K_DEV), :], kp.at[pl.ds(2 * K_DEV, 2 * K_DEV), :], s3_send.at[0], s3_recv.at[0],
            {"head": head, "seq": z * PLANE + xl * 2 + (1 - core)},
        )

    for c in range(CHUNKS):
        for direction in range(2):
            when(comes(direction, 2, z), trunk_copy(direction, 2, c).start)
    for copy in scalars:
        copy.wait()
    picked = (pick_ref[0] // (QH // KV)).astype(jnp.float32)
    pick_out[...] = jnp.full((16, HD), picked, jnp.float32).astype(jnp.bfloat16)
    picks[head] = pick_out[...]
    for i in range(1, NH):
        pk_copy(i).start()
    for i in range(1, NH):
        s1_copy(i).start()
    serve_leaves(1)
    for side in range(2):
        signal(greet.at[0, side], at_z(z + 2 - 4 * side))

    key_local = lax.broadcasted_iota(jnp.int32, (BLK, BLK), 0)
    query_local = lax.broadcasted_iota(jnp.int32, (BLK, BLK), 1)
    table[0] = jnp.full((BLK, BLK), NEGATIVE, jnp.float32)
    table[1] = jnp.where(key_local <= query_local, 0.0, NEGATIVE)
    table[2] = jnp.zeros((BLK, BLK), jnp.float32)

    trunk_step(2)
    for side in range(2):
        pl.semaphore_wait(greet.at[0, side], 1)
    for side in range(2):
        signal(greet.at[1, side], at_z(z + 4 - 8 * side))
    own_k.wait()
    for i in range(1, NH):
        pk_arrival(i).wait_recv()
        s1_arrival(i).wait_recv()
    pieces = [recv1[m].astype(jnp.float32) for m in range(NH)]
    for g in range(NH):
        wanted = picks[g].astype(jnp.float32)[0:8]
        wanted = jnp.concatenate([wanted] * (PIECE // 8), axis=0)
        chosen = pieces[0]
        for m in range(1, NH):
            chosen = jnp.where(wanted == float(m), pieces[m], chosen)
        stage2[g] = chosen.astype(jnp.bfloat16)
    for gi, xo in s2_pairs:
        s2_copy(gi, xo).start()
    kp[pl.ds(xl * K_DEV + head * PIECE, PIECE), :] = stage2[head]
    trunk_step(4)
    for side in range(2):
        pl.semaphore_wait(greet.at[1, side], 1)
    signal(greet.at[2, 0], at_pair(0, 1))
    wait_leaves(1)
    own_q.wait()

    @pl.when(z >= FORWARD)
    def _():
        for c in range(CHUNKS):
            serve(6, c)
        serve_leaves(7)

    for gi, xo in s2_pairs:
        s2_arrival(gi, xo).wait_recv()
    s3_copy().start()

    offset = off_ref[0]
    far = wrap(z + HALF)

    def pr_copy(r):
        return remote(probs.at[wrap(z + HALF + r)], prob_in.at[z], pr_send.at[r], pr_recv.at[r], at_z(z + r))

    def tp_copy(r):
        return remote(tops.at[wrap(z + HALF + r)], top_in.at[z], tp_send.at[r], tp_recv.at[r], at_z(z + r))

    def pr_arrival(r):
        source = wrap(z - r)
        return remote(probs.at[source], prob_in.at[source], pr_send.at[r], pr_recv.at[r], at_z(z - r))

    def tp_arrival(r):
        source = wrap(z - r)
        return remote(tops.at[source], top_in.at[source], tp_send.at[r], tp_recv.at[r], at_z(z - r))

    first = lax.broadcasted_iota(jnp.int32, (ROWS, BLK), 0) < PKB

    def signed_of(item):
        d = (item + 1) // 2
        return jnp.where(lax.rem(item, 2) == 1, -d, d)

    def scores(item, lo, hi, masked=True):
        slot = wrap(z + signed_of(item))
        q = qall[slot]
        for kb in range(lo, hi):
            s = lax.dot_general(
                kp[kb * BLK:(kb + 1) * BLK, :], q, (((1,), (1,)), ((), ())),
                preferred_element_type=jnp.float32,
            )
            owner_core = core if kb < PKB // 2 else 1 - core
            place = z * PKB + (kb // KBD % 2 * 2 + owner_core) * KBD + kb % KBD
            for j in range(2):
                ahead = slot * 8 + cls * 2 + j + offset - place
                sj = s[:, j * BLK:(j + 1) * BLK]
                if masked:
                    sj = sj + table[jnp.clip(ahead + 1, 0, 2)]
                top = jnp.max(sj, axis=0, keepdims=True)
                row = j * PKB + kb
                maxes[item, row:row + 1, :] = top
                raw[item, row:row + 1, :] = jnp.sum(jnp.exp2((sj - top) * SCALE2), axis=0, keepdims=True)

    def close(item, slot):
        every = maxes[item]
        top0 = jnp.max(jnp.where(first, every, NEGATIVE), axis=0, keepdims=True)
        top1 = jnp.max(jnp.where(first, NEGATIVE, every), axis=0, keepdims=True)
        tops[slot, 0:1, :] = top0
        tops[slot, 1:2, :] = top1
        probs[slot] = raw[item] * jnp.exp2((every - jnp.where(first, top0, top1)) * SCALE2)

    def send_sums(item):
        r = HALF + signed_of(item)
        pr_copy(r).start()
        tp_copy(r).start()

    def wanted_item(item):
        return meets(wrap(z + signed_of(item)), z)

    def early(item, unused):
        when(wanted_item(item), lambda: scores(item, 0, PKB // 2))
        return unused

    def slot_of(item):
        return wrap(z + signed_of(item))

    def step(item, lo, closed=False):
        before = jnp.maximum(item - 1, 0)
        now, ended = wanted_item(item), wanted_item(before)
        ended = jnp.logical_and(ended, jnp.logical_not(closed))

        whole = PKB * (z + 1) <= QBD * slot_of(item) + 2 * cls

        @pl.when(jnp.logical_and(now, whole))
        def _():
            close(before, jnp.where(closed, NZ, slot_of(before)))
            scores(item, lo, PKB, False)

        @pl.when(jnp.logical_and(now, jnp.logical_not(whole)))
        def _():
            close(before, jnp.where(closed, NZ, slot_of(before)))
            scores(item, lo, PKB)

        when(jnp.logical_and(jnp.logical_not(now), ended), lambda: close(before, slot_of(before)))
        when(jnp.logical_and(ended, item >= 1), lambda: send_sums(before))

    def middle(item, unused):
        serving = jnp.logical_and(item >= 1, item < 1 + CHUNKS)
        when(jnp.logical_and(serving, z < FORWARD), lambda: serve(6, item - 1))
        step(item, PKB // 2)
        return unused

    def late(item, unused):
        @pl.when(item == EARLY)
        def _():
            when(z < FORWARD, lambda: serve_leaves(7))
            wait_leaves(3)

        waits = jnp.logical_or(item == 9, jnp.logical_or(item == 13, item == 15))

        @pl.when(jnp.logical_and(waits, wanted_item(item - 1)))
        def _():
            close(item - 1, slot_of(item - 1))
            send_sums(item - 1)

        @pl.when(item == 9)
        def _():
            wait_leaves(5)

        when(item == 13, lambda: wait_leaves(7))

        @pl.when(jnp.logical_and(item == 15, far >= HALF))
        def _():
            for c in range(CHUNKS):
                trunk_arrival(c * 2 // CHUNKS, HALF, c).wait_recv()

        step(item, 0, waits)
        return unused

    lax.fori_loop(0, EARLY, early, 0)
    s3_copy().wait_recv()
    lax.fori_loop(0, EARLY, middle, 0)
    lax.fori_loop(EARLY, 2 * HALF, late, 0)

    def no_sums(source):
        prob_in[source] = jnp.zeros((ROWS, BLK), jnp.float32)
        top_in[source] = jnp.full((2, BLK), NEGATIVE, jnp.float32)

    @pl.when(meets(far, z))
    def _():
        close(2 * HALF - 1, far)
        prob_in[z] = probs[far]
        top_in[z] = tops[far]

    when(jnp.logical_not(meets(far, z)), lambda: no_sums(z))
    for direction in range(2):
        for d in range(2, HALF, 2):
            for c in range(CHUNKS):
                piece = wrap(z - sign_of(direction) * (d - 2))
                when(comes(direction, d, piece), trunk_copy(direction, d, c).wait_send)
        for d in range(1, HALF, 2):
            piece = wrap(z - sign_of(direction) * (d - 1))
            when(comes(direction, d, piece), leaf_copy(direction, d).wait_send)
    for i in range(1, NH):
        pk_copy(i).wait_send()
        s1_copy(i).wait_send()
    for gi, xo in s2_pairs:
        s2_copy(gi, xo).wait_send()
    s3_copy().wait_send()
    for r in range(1, NZ):
        source = wrap(z - r)
        sent = meets(far, source)

        @pl.when(sent)
        def _():
            tp_arrival(r).wait_recv()
            pr_arrival(r).wait_recv()

        when(jnp.logical_not(sent), lambda: no_sums(source))
    each = top_in[...]
    top = jnp.max(each, axis=0, keepdims=True)
    factor = jnp.exp2((each - top) * SCALE2)
    total = jnp.zeros((ROWS, BLK), jnp.float32)
    for source in range(NZ):
        part = prob_in[source] * jnp.where(first, factor[source, 0:1], factor[source, 1:2])
        total = total + part
        weighted[source * ROWS:(source + 1) * ROWS, :] = part
    sum0 = jnp.sum(jnp.where(first, total, 0.0), axis=0, keepdims=True)
    sum1 = jnp.sum(jnp.where(first, 0.0, total), axis=0, keepdims=True)
    inverse = 1.0 / jnp.where(lax.broadcasted_iota(jnp.int32, (8, BLK), 0) == 0, sum0, sum1)
    mass = lax.dot_general(
        inverse, weighted[...], (((1,), (1,)), ((), ())),
        precision=lax.Precision.HIGHEST, preferred_element_type=jnp.float32,
    )
    column = lax.broadcasted_iota(jnp.int32, (1, NZ * ROWS), 1)
    mass_out[...] = jnp.where(lax.rem(column, ROWS) < PKB, mass[0:1], mass[1:2])
    mass_in[xl, far] = mass_out[...]

    def at_line(xo, r):
        return {"head": head, "seq": wrap(z + r) * PLANE + lax.rem(xl + xo, 2) * 2 + core}

    def ms_copy(xo, r):
        return remote(mass_out, mass_in.at[xl, far], ms_send.at[xo, r], ms_recv.at[xo, r], at_line(xo, r))

    def ms_arrival(xo, r):
        slot = mass_in.at[lax.rem(xl + xo, 2), wrap(z - r + HALF)]
        return remote(mass_out, slot, ms_send.at[xo, r], ms_recv.at[xo, r], at_line(xo, -r))

    crossings = [(xo, r) for d in range(HALF) for r in ((HALF - d, HALF + d) if d else (HALF,)) for xo in range(2)]
    crossings.append((1, 0))
    pl.semaphore_wait(greet.at[2, 0], 1)
    for xo, r in crossings:
        ms_copy(xo, r).start()
    wide = lax.broadcasted_iota(jnp.int32, (8, NZ * ROWS), 1)
    sub = lax.broadcasted_iota(jnp.int32, (8, NZ * ROWS), 0)
    chosen = []
    for j in range(2):
        place = jnp.full((8, NZ * ROWS), -1, jnp.int32)
        for row in range(8):
            if row % 4 < KBD:
                block = own_ref[z * PKB + (xl * 2 + row // 4) * KBD + row % 4]
                device = lax.rem(block, PKB) // KBD
                other_core = lax.rem(device + core, 2)
                inner = (other_core * 2 + device // 2) * KBD + lax.rem(block, KBD)
                lane = block // PKB * ROWS + j * PKB + inner
                place = jnp.where(sub == row, lane, place)
        chosen.append(jnp.where(wide == place, 1.0, 0.0))
    chosen = jnp.concatenate(chosen, axis=0)
    for r in range(1, NZ):
        @pl.when(meets(wrap(z + HALF + r), z))
        def _():
            pr_copy(r).wait_send()
            tp_copy(r).wait_send()

    for c in range(CHUNKS):
        direction = c * 2 // CHUNKS
        piece = wrap(z - sign_of(direction) * (HALF - 2))
        when(comes(direction, HALF, piece), trunk_copy(direction, HALF, c).wait_send)
    for xo, r in crossings:
        ms_arrival(xo, r).wait_recv()
    spread = jnp.concatenate(
        [
            jnp.where(sub == 0, jnp.broadcast_to(mass_in[x, piece], (8, NZ * ROWS)), 0.0)
            for x in range(2) for piece in range(NZ)
        ],
        axis=0,
    )
    rows = lax.dot_general(
        chosen, spread, (((1,), (1,)), ((), ())),
        precision=lax.Precision.HIGHEST, preferred_element_type=jnp.float32,
    )
    rows = rows[0:8] + pltpu.roll(rows[8:16], 1, 1)
    rows = pltpu.roll(rows[:, 0:BLK], 2 * core, 1) + pltpu.roll(rows[:, BLK:2 * BLK], 4 + 2 * core, 1)
    for c in range(2):
        plane_out[c] = rows[4 * c:4 * c + 4]
    plane_in[core] = plane_out[core]

    def pe_copy():
        return remote(
            plane_out.at[1 - core], plane_in.at[core], pe_send.at[0], pe_recv.at[0],
            {"head": head, "seq": z * PLANE + xl * 2 + (1 - core)},
        )

    def pe_arrival():
        return remote(
            plane_out.at[1 - core], plane_in.at[1 - core], pe_send.at[0], pe_recv.at[0],
            {"head": head, "seq": z * PLANE + xl * 2 + (1 - core)},
        )

    pe_copy().start()
    for xo, r in crossings:
        ms_copy(xo, r).wait_send()
    pe_arrival().wait_recv()
    final = plane_in[0] + plane_in[1]
    o_ref[0] = final[0:KBD]
    pe_copy().wait_send()


def body(queries, keys, head_pick, block_offset, owner_map):
    vmem = pl.BlockSpec(memory_space=pltpu.VMEM)
    hbm = pl.BlockSpec(memory_space=pl.ANY)
    f32, bf16 = jnp.float32, jnp.bfloat16
    dma = pltpu.SemaphoreType.DMA
    return pl.pallas_call(
        kernel,
        out_shape=jax.ShapeDtypeStruct((1, KBD, BLK), f32),
        in_specs=[hbm] * 5,
        out_specs=vmem,
        scratch_shapes=[
            pltpu.VMEM((NZ, Q_DEV, HD), bf16),
            pltpu.VMEM((PLANE * K_DEV, HD), bf16),
            pltpu.VMEM((16, HD), bf16),
            pltpu.VMEM((NH, 16, HD), bf16),
            pltpu.VMEM((NH, PIECE, HD), bf16),
            pltpu.VMEM((NH, PIECE, HD), bf16),
            pltpu.VMEM((3, BLK, BLK), f32),
            pltpu.VMEM((NZ + 1, ROWS, BLK), f32),
            pltpu.VMEM((NZ + 1, 2, BLK), f32),
            pltpu.VMEM((NZ, ROWS, BLK), f32),
            pltpu.VMEM((NZ, ROWS, BLK), f32),
            pltpu.VMEM((NZ, ROWS, BLK), f32),
            pltpu.VMEM((NZ, 2, BLK), f32),
            pltpu.VMEM((NZ * ROWS, BLK), f32),
            pltpu.VMEM((1, NZ * ROWS), f32),
            pltpu.VMEM((2, NZ, 1, NZ * ROWS), f32),
            pltpu.VMEM((2, 4, BLK), f32),
            pltpu.VMEM((2, 4, BLK), f32),
            pltpu.SMEM((1,), jnp.int32),
            pltpu.SMEM((1,), jnp.int32),
            pltpu.SMEM((NZ * PKB,), jnp.int32),
            dma((5,)), pltpu.SemaphoreType.REGULAR((3, 2)),
            dma((2, HALF // 2, CHUNKS)), dma((2, HALF // 2, CHUNKS)),
            dma((2, HALF // 2)), dma((2, HALF // 2)),
            dma((NH,)), dma((NH,)),
            dma((NH,)), dma((NH,)),
            dma((NH, 2)), dma((NH, 2)),
            dma((1,)), dma((1,)),
            dma((NZ,)), dma((NZ,)),
            dma((NZ,)), dma((NZ,)),
            dma((2, NZ)), dma((2, NZ)),
            dma((1,)), dma((1,)),
        ],
        compiler_params=pltpu.CompilerParams(
            collective_id=0, has_side_effects=True, vmem_limit_bytes=60 * 1024 * 1024
        ),
        cost_estimate=pl.CostEstimate(flops=1610612736, bytes_accessed=165000, transcendentals=6291456),
    )(queries[0], keys[0], head_pick, block_offset, owner_map)


def solution(mesh):
    return jax.shard_map(
        body,
        mesh=mesh,
        in_specs=(P("head", "seq", None), P("head", "seq", None), P("head"), P("head"), P()),
        out_specs=P("head", "seq", None),
        check_vma=False,
    )
```
